32 devices in a mesh: parts: 2 (over x), view: 8 (over z, y), slab: 2 (over core).
Axes of the slice: x: 2, y: 2, z: 4, core: 2. Of those that a mesh axis runs over, the one named last changes fastest.
Arguments:
- activity: bfloat16 [128, 32, 256], P(('parts', 'view'), 'slab'), parts along dimension 0, may hold values from 0.6 to 11.2
- histo_counts: int32 [32, 64, 32, 256], P(('parts', 'view'), None, 'slab'), parts along dimension 0, may hold values from 0 to 22
- background: bfloat16 [32, 32, 256], P(('parts', 'view'), 'slab'), parts along dimension 0, may hold values from 0.5 to 2
- blur_values: bfloat16 [16, 3, 256, 32], P('view'), may hold values from 0.0041503906 to 0.020751953
- band_start: int32 [16, 3, 256], P('view'), may hold values from 0 to 224, as said below
Outputs:
- gradient: float32 [128, 32, 256], P(('parts', 'view'), 'slab'), parts along dimension 0
The draws below stay inside these ranges and needn't reach their ends.
There are 2 independent parts, one for each index of `parts`. The reference program is written for one: setup_inputs(seed, part) draws one part's arguments, and reference() takes and returns one part's arrays. A program takes and returns all parts, laid end to end along the dimension named above; an argument that names none is the same for every part. Nothing has to cross between parts.
Inputs may be any that keep to these rules, and one draw needn't show every extreme that they name: Each band lies inside the matrix: columns band_start to band_start + 31.
All inputs are finite; a program needn't handle non-finite values.
Results may differ from the reference program's by a relative error of at most 0.0003.
Values may be sent and summed in bfloat16 or wider, within the bound.
No kernel may reach another device: no remote copies, remote signals or barrier semaphores. Data moves between devices by JAX's collectives and lax.ppermute only.
A program may use at most 64 MiB of HBM per device.

```python
import math
import jax
import jax.numpy as jnp
from jax import lax

NX = 256
BAND = 32
TAPS = 3
NY = 64
NZ = 32
VIEWS = 16


def level_grid(key):
    keyed = jax.random.fold_in(key, 11)
    levels = jax.random.randint(keyed, (NY, NZ), 0, 7)
    return levels.at[0, 0].set(6).astype(jnp.int32)


def draw_activity(key, part):
    levels = level_grid(key)
    scales = jnp.exp2(levels.astype(jnp.float32) * 0.5)
    uniform_part = jax.random.uniform(jax.random.fold_in(key, 13), (NY, NZ, NX), jnp.float32)
    factor = 0.6 + 0.8 * uniform_part
    return (scales[:, :, None] * factor).astype(jnp.bfloat16)


def draw_histo_counts(key, part):
    levels = level_grid(key)
    table = jnp.array([2, 3, 4, 5, 6, 8, 11], jnp.int32)
    means = table[levels]
    upper = 2 * means[None, :, :, None] + 1
    counts = jax.random.randint(jax.random.fold_in(key, 17), (VIEWS, NY, NZ, NX), 0, upper)
    counts = counts.at[0, 0, 0, 0].set(22)
    counts = counts.at[0, 0, 0, 1].set(0)
    return counts.astype(jnp.int32)


def draw_band_start(key, part):
    keyed = jax.random.fold_in(key, 7)
    first_key, second_key = jax.random.split(keyed)
    reach = max(BAND // 4, 1)
    offsets = jax.random.randint(first_key, (VIEWS, TAPS, 1), -reach, reach + 1)
    jitters = jax.random.randint(second_key, (VIEWS, TAPS, NX), -1, 2)
    positions = jnp.arange(NX, dtype=jnp.int32)[None, None, :]
    return jnp.clip(positions - BAND // 2 + offsets + jitters, 0, NX - BAND).astype(jnp.int32)


def level_of(rng, dims, shards, smallest, largest):
    level = 1.0
    for axis_at, shards_of in shards:
        heights = jax.random.uniform(jax.random.fold_in(jax.random.fold_in(rng, 6), axis_at), (shards_of,), jnp.float32, smallest / len(shards), largest / len(shards))
        level = level * jnp.repeat(jnp.exp(heights), dims[axis_at] // shards_of).reshape((-1,) + (1,) * (len(dims) - 1 - axis_at))
    return level


def setup_inputs(seed: int = 0, part: int = 0) -> dict:
    seeds = jax.random.split(jax.random.key(seed), 6)
    part_keys = jax.random.split(jax.random.fold_in(seeds[5], part), 6)
    return {
        "activity": draw_activity(jax.random.fold_in(jax.random.fold_in(seeds[5], part), 71), part),
        "histo_counts": draw_histo_counts(jax.random.fold_in(jax.random.fold_in(seeds[5], part), 71), part),
        "background": jnp.clip(jnp.exp(math.log(2.0) - 1.3862944 * jax.random.uniform(part_keys[2], (VIEWS, NZ, NX), jnp.float32) ** level_of(part_keys[2], (VIEWS, NZ, NX), ((0, 8), (1, 2)), -0.2, 0.2)), 0.5, 2.0).astype(jnp.bfloat16),
        "blur_values": jnp.clip(0.0041503906 + 0.016601562 * jax.random.uniform(seeds[3], (VIEWS, TAPS, NX, BAND), jnp.float32) ** level_of(seeds[3], (VIEWS, TAPS, NX, BAND), ((0, 8),), -0.2, 0.2), 0.0041503906, 0.020751953).astype(jnp.bfloat16),
        "band_start": draw_band_start(jax.random.fold_in(seeds[5], 71), part),
    }


def blur_matrix(band_values, band_starts):
    width_x = band_values.shape[0]
    band_width = band_values.shape[1]
    columns = jnp.arange(width_x, dtype=jnp.int32)
    distance = columns[None, :] - band_starts.astype(jnp.int32)[:, None]
    selector = (distance[:, :, None] == jnp.arange(band_width, dtype=jnp.int32)[None, None, :]).astype(jnp.float32)
    return jnp.einsum('ik,ijk->ij', band_values.astype(jnp.float32), selector).astype(jnp.bfloat16)


def view_gradient(activity, view_counts, view_background, view_values, view_starts):
    rows_y, slices, width_x = activity.shape
    matrices = [blur_matrix(view_values[tap_index], view_starts[tap_index]) for tap_index in range(3)]
    padded = jnp.pad(activity, ((0, 0), (1, 1), (0, 0)))
    summed = jnp.zeros((rows_y * slices, width_x), jnp.float32)
    for tap_index in range(3):
        shifted = padded[:, tap_index:tap_index + slices, :].reshape(-1, width_x)
        summed = summed + jnp.dot(shifted, matrices[tap_index].T, preferred_element_type=jnp.float32)
    expected = summed.reshape(rows_y, slices, width_x) + view_background.astype(jnp.float32)[None]
    ratio_bf = (view_counts.astype(jnp.float32) / expected - 1.0).astype(jnp.bfloat16)
    widened = jnp.pad(ratio_bf, ((0, 0), (1, 1), (0, 0)))
    back_sum = jnp.zeros((rows_y * slices, width_x), jnp.float32)
    for tap_index in range(3):
        shifted = widened[:, 2 - tap_index:2 - tap_index + slices, :].reshape(-1, width_x)
        back_sum = back_sum + jnp.dot(shifted, matrices[tap_index], preferred_element_type=jnp.float32)
    return back_sum.reshape(rows_y, slices, width_x)


def reference(activity, histo_counts, background, blur_values, band_start):
    def one_view(carry, inputs):
        view_counts, view_background, view_values, view_starts = inputs
        return carry + view_gradient(activity, view_counts, view_background, view_values, view_starts), None

    start_value = jnp.zeros(activity.shape, jnp.float32)
    gradient, _ = lax.scan(one_view, start_value, (histo_counts, background, blur_values, band_start))
    return gradient
```

```python
import functools

import jax
import jax.numpy as jnp
from jax import lax
from jax.experimental import pallas as pl
from jax.experimental.pallas import tpu as pltpu
from jax.sharding import PartitionSpec as P

VMEM = pl.BlockSpec(memory_space=pltpu.VMEM)
SMEM = pl.BlockSpec(memory_space=pltpu.SMEM)
BF16, F32, I32 = jnp.bfloat16, jnp.float32, jnp.int32


def build_kernel(values_ref, starts_ref, out_ref):
    views, taps, band, width = values_ref.shape
    for view in range(views):
        for tap in range(taps):
            start = starts_ref[view * taps + tap : view * taps + tap + 1, :]
            moved = jnp.concatenate(
                [values_ref[view, tap].astype(F32), jnp.zeros((8, width), F32)], axis=0
            )
            for step in (1, 2, 4):
                moved = jnp.where((start & step) != 0, pltpu.roll(moved, step, 0), moved)
            step = 8
            while step < width:
                length = moved.shape[0]
                longer = min(length + step, width)
                zeros = jnp.zeros((step, width), F32)
                down = jnp.concatenate([zeros, moved], axis=0)[:longer]
                stay = jnp.concatenate([moved, zeros], axis=0)[:longer]
                moved = jnp.where((start & step) != 0, down, stay)
                step *= 2
            out_ref[view, tap] = moved.astype(BF16)


def build(values, starts):
    views, taps, _, width = values.shape
    return pl.pallas_call(
        build_kernel,
        out_shape=jax.ShapeDtypeStruct((views, taps, width, width), BF16),
        in_specs=[VMEM, VMEM],
        out_specs=VMEM,
        cost_estimate=pl.CostEstimate(
            flops=views * taps * width * width * 8,
            bytes_accessed=views * taps * width * width * 2,
            transcendentals=0,
        ),
    )(values, starts)


def rows_kernel(groups, blocks, flags_ref, source_ref, *refs):
    taps, full, width = source_ref.shape
    ins, (outs, (ratio_ref, first_ref, last_ref)) = (
        refs[: 5 * groups],
        (refs[5 * groups : 5 * groups + blocks], refs[5 * groups + blocks :]),
    )
    rows, slices = ratio_ref.shape[1] - 0, outs[0].shape[1]
    rows = full // (slices + 2)
    main = rows * slices
    views = []
    for group in range(groups):
        counts_ref, edge_ref, back_ref, back_edge_ref, matrix_ref = ins[5 * group : 5 * group + 5]
        for view in range(counts_ref.shape[0]):
            at = len(views)
            expected = jnp.dot(source_ref[0], matrix_ref[view, 0], preferred_element_type=F32)
            for tap in range(1, taps):
                expected += jnp.dot(
                    source_ref[tap], matrix_ref[view, tap], preferred_element_type=F32
                )
            inner = expected[:main].reshape(rows, slices, width) + back_ref[view].astype(F32)[None]
            counts = counts_ref[view].astype(F32).reshape(rows, slices, width)
            ratio_ref[at, :main] = (counts / inner - 1.0).astype(BF16).reshape(main, width)
            for side in range(2):
                low = main + side * rows
                outer = (
                    expected[low : low + rows]
                    + back_edge_ref[view, side : side + 1].astype(F32)
                )
                ratio = edge_ref[view, side].astype(F32) / outer - 1.0
                ratio = jnp.where(flags_ref[side] != 0, ratio, 0.0)
                ratio_ref[at, low : low + rows] = ratio.astype(BF16)
            views.append((matrix_ref, view))

    def back(tap, start, stop):
        total = None
        for at, (matrix_ref, view) in enumerate(views):
            term = lax.dot_general(
                ratio_ref[at, start:stop],
                matrix_ref[view, tap],
                (((1,), (1,)), ((), ())),
                preferred_element_type=F32,
            )
            total = term if total is None else total + term
        return total

    first = back(0, 0, full)
    first_ref[:, :slices, :] = first[:main].reshape(rows, slices, width)
    first_ref[:, slices, :] = first[main + rows :]
    last = back(2, 0, main + rows)
    last_ref[:, 8 : 8 + slices, :] = last[:main].reshape(rows, slices, width)
    last_ref[:, 7, :] = last[main:]
    middle = back(1, 0, main).reshape(rows, slices, width)
    total = middle + first_ref[:, 1 : 1 + slices, :] + last_ref[:, 7 : 7 + slices, :]
    each = rows // blocks
    for block in range(blocks):
        outs[block][...] = total[block * each : (block + 1) * each]


def row_terms(flags, source, groups, blocks, rows, slices):
    taps, full, width = source.shape
    n_views = sum(group[0].shape[0] for group in groups)
    flops = 4 * n_views * taps * full * width * width
    return pl.pallas_call(
        functools.partial(rows_kernel, len(groups), blocks),
        out_shape=[jax.ShapeDtypeStruct((rows // blocks, slices, width), F32)] * blocks,
        in_specs=[SMEM] + [VMEM] * (1 + 5 * len(groups)),
        out_specs=[VMEM] * blocks,
        scratch_shapes=[
            pltpu.VMEM((n_views, full, width), BF16),
            pltpu.VMEM((rows, slices + 8, width), F32),
            pltpu.VMEM((rows, slices + 8, width), F32),
        ],
        compiler_params=pltpu.CompilerParams(vmem_limit_bytes=24 * 1024 * 1024),
        cost_estimate=pl.CostEstimate(flops=flops, bytes_accessed=4 * full * width, transcendentals=0),
    )(flags, source, *[x for group in groups for x in group])


def per_device(activity, histo_counts, background, blur_values, band_start):
    each, slices, width = activity.shape
    views, taps, _, band = blur_values.shape
    n_slab, slab = lax.axis_size("slab"), lax.axis_index("slab")
    n_view, at_view = lax.axis_size("view"), lax.axis_index("view")
    pairs = 2 if n_view % 2 == 0 else 1
    line = n_view // pairs
    at_line, side = at_view // pairs, at_view % pairs
    xor = line & (line - 1) == 0

    def peer(at, k):
        return at ^ k if xor else (at + k) % line

    def across(k, towards):
        moves = [(i, peer(i // pairs, k) * pairs + i % pairs) for i in range(n_view)]
        return moves if towards else [(j, i) for i, j in moves]

    other = [(i, i ^ 1) for i in range(n_view)]

    counts = histo_counts.reshape(views, line, pairs, each, slices, width)

    def edges(at, length):
        pick = lambda x, axis, n: lax.slice_in_dim(
            x, 0 if at == 0 else slices - n, n if at == 0 else slices, axis=axis
        )
        return jnp.concatenate(
            [
                pick(activity, 1, 2).reshape(-1, width),
                pick(counts, 4, 1).astype(BF16).reshape(-1, width),
                pick(background, 1, 1).reshape(-1, width),
            ],
            axis=0,
        )

    if n_slab == 2:
        swapped = lax.ppermute(
            jnp.where(slab == 0, edges(1, 0), edges(0, 0)), "slab", [(0, 1), (1, 0)]
        )[None]
    elif n_slab > 2:
        up = [(i, i + 1) for i in range(n_slab - 1)]
        swapped = jnp.stack(
            [
                lax.ppermute(edges(1, 0), "slab", up),
                lax.ppermute(edges(0, 0), "slab", [(j, i) for i, j in up]),
            ]
        )
    else:
        swapped = jnp.zeros((1, each * (2 + views * line * pairs) + views, width), BF16)
    n_edges = swapped.shape[0]
    has = jnp.stack([slab > 0, slab < n_slab - 1])

    def sides(x):
        both = jnp.concatenate([x, x], axis=0) if n_edges == 1 else x
        return jnp.where(has.reshape((2,) + (1,) * (x.ndim - 1)), both, jnp.zeros_like(both))

    cut = [2 * each, 2 * each + views * line * pairs * each]
    edge_activity = sides(swapped[:, : cut[0]].reshape(n_edges, each, 2, width))
    edge_counts = swapped[:, cut[0] : cut[1]].reshape(n_edges, views, line, pairs, each, width)
    edge_back = swapped[:, cut[1] :]

    def rows_of(x, k, of_side, axis):
        x = lax.dynamic_slice_in_dim(x, peer(at_line, k), 1, axis=axis)
        x = lax.dynamic_slice_in_dim(x, of_side, 1, axis=axis + 1)
        return x.reshape(x.shape[:axis] + x.shape[axis + 2 :])

    def gather_rows(x, ks, of_side, axis):
        return jnp.stack([rows_of(x, k, of_side, axis) for k in ks], axis=axis)

    halves = [h for h in (range(line // 2, line), range(line // 2)) if len(h)]
    values = jnp.swapaxes(blur_values, 2, 3)
    starts = band_start.reshape(views * taps, width)

    theirs = []
    if pairs == 2:
        for ks in halves:
            sent = gather_rows(counts, ks, 1 - side, 1).astype(BF16)
            theirs.append(lax.ppermute(sent, "view", other))
        edge_out = gather_rows(edge_counts, range(line), 1 - side, 2)
        exact = width <= 256
        pieces = [values.reshape(-1, width), background.reshape(-1, width), edge_back.reshape(-1, width)]
        pieces += [edge_out.reshape(-1, width)]
        if exact:
            pieces.append(starts.astype(BF16))
        sizes = [p.shape[0] for p in pieces]
        arrived = lax.ppermute(jnp.concatenate(pieces, axis=0), "view", other)
        parts, low = [], 0
        for size in sizes:
            parts.append(arrived[low : low + size])
            low += size
        their_starts = parts[4].astype(I32) if exact else lax.ppermute(starts, "view", other)

    padded = jnp.concatenate([edge_activity[0], activity, edge_activity[1]], axis=1)
    blocks = [padded] + [
        lax.ppermute(padded, "view", across(k, False)) for k in range(1, line)
    ]

    mine_matrices = build(values, starts)
    if pairs == 2:
        their_matrices = build(parts[0].reshape(values.shape), their_starts)

    flags = has.astype(I32)
    back_edges = lambda x: jnp.swapaxes(sides(x.reshape(n_edges, views, width)), 0, 1)
    terms = {}
    for at, ks in enumerate(halves):
        rows = len(ks) * each
        taken = jnp.concatenate([blocks[k] for k in ks], axis=0)
        source = jnp.stack(
            [
                jnp.concatenate(
                    [
                        taken[:, 1 + t : 1 + t + slices].reshape(-1, width),
                        taken[:, t],
                        taken[:, slices + 1 + t],
                    ],
                    axis=0,
                )
                for t in range(taps)
            ]
        )

        def group(rows_counts, edge, back, back_edge, matrices):
            edge = jnp.moveaxis(sides(edge), 0, 1).reshape(views, 2, rows, width)
            return (
                rows_counts.reshape(views, rows * slices, width),
                edge,
                back.reshape(views, slices, width),
                back_edges(back_edge),
                matrices,
            )

        groups = [
            group(
                gather_rows(counts, ks, side, 1).astype(BF16),
                gather_rows(edge_counts, ks, side, 2),
                background,
                edge_back,
                mine_matrices,
            )
        ]
        if pairs == 2:
            edge_in = parts[3].reshape(n_edges, views, line, each, width)[:, :, ks[0] : ks[-1] + 1]
            groups.append(group(theirs[at], edge_in, parts[1], parts[2], their_matrices))
        outs = row_terms(flags, source, groups, len(ks), rows, slices)
        terms.update(zip(ks, outs))
    total = terms[0]
    for k in reversed(range(1, line)):
        total = total + lax.ppermute(terms[k], "view", across(k, True))
    return total


def solution(mesh):
    placed = (
        P(("parts", "view"), "slab", None),
        P(("parts", "view"), None, "slab", None),
        P(("parts", "view"), "slab", None),
        P("view", None, None, None),
        P("view", None, None),
    )
    return jax.shard_map(
        per_device,
        mesh=mesh,
        in_specs=placed,
        out_specs=P(("parts", "view"), "slab", None),
        check_vma=False,
    )
```

```python
import functools

import jax
import jax.numpy as jnp
from jax import lax
from jax.experimental import pallas as pl
from jax.experimental.pallas import tpu as pltpu
from jax.sharding import PartitionSpec as P

VMEM = pl.BlockSpec(memory_space=pltpu.VMEM)
BF16, F32, I32 = jnp.bfloat16, jnp.float32, jnp.int32


def padded_16(rows):
    return -(-rows // 16) * 16


class Plan:
    def __init__(self, activity, histo_counts, blur_values):
        self.each, self.slices, self.width = activity.shape
        self.views, self.taps, _, self.band = blur_values.shape
        self.n_slab = lax.axis_size("slab")
        self.n_view = lax.axis_size("view")
        self.pairs = 2 if self.n_view % 2 == 0 else 1
        self.line = self.n_view // self.pairs
        self.block = self.each * self.slices
        self.n_edges = 2 if self.n_slab > 2 else 1
        halves = (range(self.line // 2, self.line), range(self.line // 2))
        self.halves = [h for h in halves if len(h)]
        self.edge_counts = 2 * self.each
        self.edge_back = self.edge_counts + self.views * self.n_view * self.each
        self.edge_rows = self.edge_back + padded_16(self.views)
        self.bands = self.views * self.taps * self.band
        self.starts = self.bands + self.views * self.slices
        self.param_rows = self.starts + padded_16(2 * self.views * self.taps)
        self.first_counts = self.param_rows
        self.first_edges = self.first_counts + self.views * len(self.halves[0]) * self.block
        self.edges_each = self.views * self.line * self.each
        self.first_back = self.first_edges + self.n_edges * self.edges_each
        self.first_rows = self.first_back + self.n_edges * padded_16(self.views)

    def peer(self, at, k):
        xor = self.line & (self.line - 1) == 0
        return at ^ k if xor else (at + k) % self.line

    def across(self, k, towards):
        g = self.pairs
        moves = [(i, self.peer(i // g, k) * g + i % g) for i in range(self.n_view)]
        return moves if towards else [(j, i) for i, j in moves]

    def valid(self):
        slab = lax.axis_index("slab")
        return (slab > 0, slab < self.n_slab - 1)


def call(kernel, outs, *args, scratch=(), flops=0, specs=None):
    size = lambda xs: sum(x.size * x.dtype.itemsize for x in xs)
    return pl.pallas_call(
        kernel,
        out_shape=outs,
        in_specs=specs or [VMEM] * len(args),
        out_specs=[VMEM] * len(outs),
        scratch_shapes=list(scratch),
        compiler_params=pltpu.CompilerParams(vmem_limit_bytes=24 * 1024 * 1024),
        cost_estimate=pl.CostEstimate(
            flops=flops, bytes_accessed=size(args) + size(outs), transcendentals=0
        ),
    )(*args)


def pack_kernel(p, counts_ref, activity_ref, back_ref, edges_ref, tiles_ref, active_ref, backs_ref, sems):
    slab = lax.axis_index("slab")
    last, tile = p.slices - 1, min(8, p.slices)
    copies = [
        pltpu.make_async_copy(activity_ref, active_ref, sems.at[0]),
        pltpu.make_async_copy(back_ref, backs_ref, sems.at[1]),
    ]
    for slot in range(p.n_edges):
        first = (slot == 0) if p.n_edges == 2 else (slab == 0)
        low = jnp.where(first, p.slices - tile, 0)
        copies.append(
            pltpu.make_async_copy(
                counts_ref.at[:, :, :, pl.ds(pl.multiple_of(low, tile), tile), :],
                tiles_ref.at[slot],
                sems.at[2 + slot],
            )
        )
    for copy in copies:
        copy.start()
    copies[0].wait()
    copies[1].wait()
    activity = active_ref[...].astype(F32)
    back = backs_ref[...].astype(F32)
    for slot in range(p.n_edges):
        copies[2 + slot].wait()

        def edge(high, low):
            if p.n_edges == 2:
                return high if slot == 0 else low
            return jnp.where(slab == 0, high, low)

        for j in range(2):
            edges_ref[slot, j * p.each : (j + 1) * p.each] = edge(
                activity[:, last - 1 + j, :], activity[:, j, :]
            )
        for v in range(p.views):
            for r in range(p.n_view):
                at = p.edge_counts + (v * p.n_view + r) * p.each
                edges_ref[slot, at : at + p.each] = edge(
                    tiles_ref[slot, v, r, :, tile - 1, :], tiles_ref[slot, v, r, :, 0, :]
                ).astype(F32)
            edges_ref[slot, p.edge_back + v : p.edge_back + v + 1] = edge(
                back[v, last : last + 1], back[v, 0:1]
            )
        tail = p.edge_rows - p.edge_back - p.views
        if tail:
            edges_ref[slot, p.edge_back + p.views :] = jnp.zeros((tail, p.width), F32)


def send_kernel(p, edges_ref, counts_ref, activity_ref, back_ref, values_ref, starts_ref, payload_ref, *outs):
    at = lax.axis_index("view")
    at_line, side = at // p.pairs, at % p.pairs
    payload_ref[: p.block] = activity_ref[...].reshape(p.block, p.width)
    for high, valid in enumerate(p.valid()):
        edge = edges_ref[min(high, p.n_edges - 1), : 2 * p.each]
        low = p.block + high * 2 * p.each
        payload_ref[low : low + 2 * p.each] = jnp.where(valid, edge, 0.0).astype(BF16)
    if p.pairs == 1:
        return
    (out,) = outs
    out[: p.bands] = values_ref[...].reshape(p.bands, p.width)
    out[p.bands : p.starts] = back_ref[...].reshape(p.views * p.slices, p.width)
    starts = starts_ref[...]
    pieces = [lax.shift_right_logical(starts, 7), starts & 127]
    tail = p.param_rows - p.starts - 2 * p.views * p.taps
    if tail:
        pieces.append(jnp.zeros((tail, p.width), I32))
    out[p.starts : p.param_rows] = jnp.concatenate(pieces, axis=0).astype(F32).astype(BF16)
    copy_counts(p, p.halves[0], counts_ref, out, p.first_counts)
    for e in range(p.n_edges):
        pieces = []
        for v in range(p.views):
            for k in range(p.line):
                row = p.peer(at_line, k) * 2 + (1 - side)
                start = p.edge_counts + (v * p.n_view + row) * p.each
                pieces.append(edges_ref[e, pl.ds(pl.multiple_of(start, p.each), p.each), :])
        low = p.first_edges + e * p.edges_each
        out[low : low + p.edges_each] = jnp.concatenate(pieces, axis=0).astype(BF16)
        low = p.first_back + e * padded_16(p.views)
        out[low : low + padded_16(p.views)] = edges_ref[
            e, p.edge_back : p.edge_back + padded_16(p.views)
        ].astype(BF16)


def copy_counts(p, ks, counts_ref, out, base):
    at = lax.axis_index("view")
    for v in range(p.views):
        for i, k in enumerate(ks):
            row = p.peer(at // p.pairs, k) * 2 + 1 - at % p.pairs
            low = base + (v * len(ks) + i) * p.block
            counts = counts_ref[v, row].astype(F32).astype(BF16)
            out[low : low + p.block] = counts.reshape(p.block, p.width)


def place_bands(values, start):
    width = values.shape[1]
    moved = jnp.concatenate([values, jnp.zeros((8, width), F32)], axis=0)
    for step in (1, 2, 4):
        moved = jnp.where((start & step) != 0, pltpu.roll(moved, step, 0), moved)
    step = 8
    while step < width:
        longer = min(moved.shape[0] + step, width)
        zeros = jnp.zeros((step, width), F32)
        down = jnp.concatenate([zeros, moved], axis=0)[:longer]
        stay = jnp.concatenate([moved, zeros], axis=0)[:longer]
        moved = jnp.where((start & step) != 0, down, stay)
        step *= 2
    return moved.astype(BF16)


def own_kernel(p, values_ref, starts_ref, counts_ref, *refs):
    blocks, outs, lifted_ref = refs[: p.line], refs[p.line : -1], refs[-1]
    matrix_ref, sources = outs[0], outs[1 : 1 + len(p.halves)]
    if p.pairs == 2:
        for ks, out in zip(p.halves[1:], outs[1 + len(p.halves) :]):
            copy_counts(p, ks, counts_ref, out, 0)
    for v in range(p.views):
        for t in range(p.taps):
            at = v * p.taps + t
            matrix_ref[v, t] = place_bands(
                values_ref[v, t].astype(F32), starts_ref[at : at + 1]
            )
    for ks, source_ref in zip(p.halves, sources):
        rows = len(ks) * p.each
        for i, k in enumerate(ks):
            low = i * p.each
            lifted_ref[low : low + p.each, 8 : 8 + p.slices, :] = (
                blocks[k][: p.block].astype(F32).reshape(p.each, p.slices, p.width)
            )
            edges = blocks[k][p.block :].astype(F32)
            for high in range(2):
                for j in range(2):
                    lifted_ref[low : low + p.each, (8 + p.slices if high else 6) + j, :] = edges[
                        (2 * high + j) * p.each : (2 * high + j + 1) * p.each
                    ]
        main = rows * p.slices
        for t in range(p.taps):
            source_ref[t, :main] = (
                lifted_ref[:rows, 7 + t : 7 + t + p.slices, :].astype(BF16).reshape(main, p.width)
            )
            source_ref[t, main:] = jnp.concatenate(
                [lifted_ref[:rows, 6 + t, :], lifted_ref[:rows, 7 + p.slices + t, :]], axis=0
            ).astype(BF16)


def their_kernel(p, params_ref, matrix_ref):
    starts = params_ref[p.starts : p.param_rows].astype(F32).astype(I32)
    n = p.views * p.taps
    starts = starts[:n] * 128 + starts[n : 2 * n]
    for v in range(p.views):
        for t in range(p.taps):
            at = v * p.taps + t
            values = params_ref[at * p.band : (at + 1) * p.band].astype(F32)
            matrix_ref[v, t] = place_bands(values, starts[at : at + 1])


def rows_kernel(p, half, source_ref, counts_ref, edges_ref, back_ref, matrix_ref, *refs):
    ks = p.halves[half]
    if p.pairs == 2:
        (their_ref, first_ref, their_matrix_ref), refs = refs[:3], refs[3:]
        base = p.first_counts if half == 0 else 0
    outs, (ratio_ref, up_ref, down_ref) = refs[: len(ks)], refs[len(ks) :]
    at = lax.axis_index("view")
    at_line, side = at // p.pairs, at % p.pairs
    rows = len(ks) * p.each
    main, full = rows * p.slices, rows * (p.slices + 2)
    views = []

    def view(matrix_ref, v, counts, back, edges, edge_backs):
        expected = None
        for t in range(p.taps):
            term = jnp.dot(source_ref[t], matrix_ref[v, t], preferred_element_type=F32)
            expected = term if expected is None else expected + term
        inner = expected[:main].reshape(rows, p.slices, p.width) + back[None]
        ratio = counts / inner - 1.0
        n = len(views)
        ratio_ref[n, :main] = ratio.astype(BF16).reshape(main, p.width)
        for high, valid in enumerate(p.valid()):
            low = main + high * rows
            e = min(high, p.n_edges - 1)
            ratio = edges[e] / (expected[low : low + rows] + edge_backs[e]) - 1.0
            ratio_ref[n, low : low + rows] = jnp.where(valid, ratio, 0.0).astype(BF16)
        views.append((matrix_ref, v))

    for v in range(p.views):
        counts, edges, edge_backs = [], [], []
        for k in ks:
            counts.append(counts_ref[v, p.peer(at_line, k) * p.pairs + side])
        for e in range(p.n_edges):
            pieces = []
            for k in ks:
                row = p.peer(at_line, k) * p.pairs + side
                start = p.edge_counts + (v * p.n_view + row) * p.each
                pieces.append(edges_ref[e, pl.ds(pl.multiple_of(start, p.each), p.each), :])
            edges.append(jnp.concatenate(pieces, axis=0))
            edge_backs.append(edges_ref[e, p.edge_back + v : p.edge_back + v + 1])
        counts = jnp.concatenate(counts, axis=0).astype(F32)
        view(matrix_ref, v, counts, back_ref[v].astype(F32), edges, edge_backs)
    if p.pairs == 2:
        for v in range(p.views):
            edges, edge_backs = [], []
            for e in range(p.n_edges):
                start = p.first_edges + e * p.edges_each + (v * p.line + ks[0]) * p.each
                edges.append(first_ref[start : start + rows].astype(F32))
                start = p.first_back + e * padded_16(p.views)
                backs = first_ref[start : start + padded_16(p.views)].astype(F32)
                edge_backs.append(backs[v : v + 1])
            counts = their_ref[base + v * main : base + (v + 1) * main].astype(F32)
            back = first_ref[p.bands + v * p.slices : p.bands + (v + 1) * p.slices].astype(F32)
            view(
                their_matrix_ref,
                v,
                counts.reshape(rows, p.slices, p.width),
                back,
                edges,
                edge_backs,
            )

    def project(tap, stop):
        total = None
        for n, (matrix_ref, v) in enumerate(views):
            term = lax.dot_general(
                ratio_ref[n, :stop],
                matrix_ref[v, tap],
                (((1,), (1,)), ((), ())),
                preferred_element_type=F32,
            )
            total = term if total is None else total + term
        return total

    part = project(0, full)
    up_ref[:, : p.slices, :] = part[:main].reshape(rows, p.slices, p.width)
    up_ref[:, p.slices, :] = part[main + rows :]
    part = project(2, main + rows)
    down_ref[:, 8 : 8 + p.slices, :] = part[:main].reshape(rows, p.slices, p.width)
    down_ref[:, 7, :] = part[main:]
    total = project(1, main).reshape(rows, p.slices, p.width)
    total = total + up_ref[:, 1 : 1 + p.slices, :] + down_ref[:, 7 : 7 + p.slices, :]
    for i, out in enumerate(outs):
        out[...] = total[i * p.each : (i + 1) * p.each]


def per_device(activity, histo_counts, background, blur_values, band_start):
    p = Plan(activity, histo_counts, blur_values)
    shape = jax.ShapeDtypeStruct
    part = lambda kernel, *static: functools.partial(kernel, p, *static)
    width = p.width
    counts = histo_counts.reshape(p.views, p.n_view, p.each, p.slices, width)
    values = jnp.swapaxes(blur_values, 2, 3)
    starts = band_start.reshape(p.views * p.taps, width)
    other = [(i, i ^ 1) for i in range(p.n_view)]

    edges = call(
        part(pack_kernel),
        [shape((p.n_edges, p.edge_rows, width), F32)],
        counts, activity, background,
        specs=[pl.BlockSpec(memory_space=pl.ANY)] * 3,
        scratch=[
            pltpu.VMEM((p.n_edges, p.views, p.n_view, p.each, min(8, p.slices), width), I32),
            pltpu.VMEM(activity.shape, BF16),
            pltpu.VMEM(background.shape, BF16),
            pltpu.SemaphoreType.DMA((2 + p.n_edges,)),
        ],
    )[0]
    if p.n_slab == 2:
        edges = lax.ppermute(edges, "slab", [(0, 1), (1, 0)])
    elif p.n_slab > 2:
        up = [(i, i + 1) for i in range(p.n_slab - 1)]
        down = [(j, i) for i, j in up]
        edges = jnp.stack([lax.ppermute(edges[0], "slab", up), lax.ppermute(edges[1], "slab", down)])
    outs = [shape((p.block + 4 * p.each, width), BF16)]
    if p.pairs == 2:
        outs.append(shape((p.first_rows, width), BF16))
    payload, *sent = call(
        part(send_kernel), outs, edges, counts, activity, background, values, starts
    )
    theirs = [lax.ppermute(x, "view", other) for x in sent]
    blocks = [payload] + [lax.ppermute(payload, "view", p.across(k, False)) for k in range(1, p.line)]

    matrices = shape((p.views, p.taps, width, width), BF16)
    most = max(len(h) for h in p.halves) * p.each
    outs = [matrices]
    outs += [shape((p.taps, len(h) * p.each * (p.slices + 2), width), BF16) for h in p.halves]
    if p.pairs == 2:
        outs += [shape((p.views * len(h) * p.block, width), BF16) for h in p.halves[1:]]
    matrix, *outs = call(
        part(own_kernel), outs, values, starts, counts, *blocks,
        scratch=[pltpu.VMEM((most, p.slices + 16, width), F32)],
    )
    sources, later = outs[: len(p.halves)], outs[len(p.halves) :]
    theirs += [lax.ppermute(x, "view", other) for x in later]
    if p.pairs == 2:
        (their_matrix,) = call(part(their_kernel), [matrices], theirs[0])

    terms = {}
    for half, ks in enumerate(p.halves):
        args = [sources[half], counts, edges, background, matrix]
        if p.pairs == 2:
            args += [theirs[half], theirs[0], their_matrix]
        rows = len(ks) * p.each
        full = rows * (p.slices + 2)
        n_views = p.views * p.pairs
        outs = call(
            part(rows_kernel, half),
            [shape((p.each, p.slices, width), F32)] * len(ks),
            *args,
            scratch=[
                pltpu.VMEM((n_views, full, width), BF16),
                pltpu.VMEM((rows, p.slices + 8, width), F32),
                pltpu.VMEM((rows, p.slices + 8, width), F32),
            ],
            flops=4 * n_views * p.taps * full * width * width,
        )
        terms.update(zip(ks, outs))
    total = terms[0]
    for k in reversed(range(1, p.line)):
        total = total + lax.ppermute(terms[k], "view", p.across(k, True))
    return total


def solution(mesh):
    placed = (
        P(("parts", "view"), "slab", None),
        P(("parts", "view"), None, "slab", None),
        P(("parts", "view"), "slab", None),
        P("view", None, None, None),
        P("view", None, None),
    )
    return jax.shard_map(
        per_device,
        mesh=mesh,
        in_specs=placed,
        out_specs=P(("parts", "view"), "slab", None),
        check_vma=False,
    )
```

```python
import functools

import jax
import jax.numpy as jnp
from jax import lax
from jax.experimental import pallas as pl
from jax.experimental.pallas import tpu as pltpu
from jax.sharding import PartitionSpec as P

VMEM = pl.BlockSpec(memory_space=pltpu.VMEM)
BF16, F32, I32 = jnp.bfloat16, jnp.float32, jnp.int32


def padded_16(rows):
    return -(-rows // 16) * 16


class Plan:
    def __init__(self, activity, histo_counts, blur_values):
        self.each, self.slices, self.width = activity.shape
        self.views, self.taps, _, self.band = blur_values.shape
        self.n_slab = lax.axis_size("slab")
        self.n_view = lax.axis_size("view")
        self.pairs = 2 if self.n_view % 2 == 0 else 1
        self.line = self.n_view // self.pairs
        self.block = self.each * self.slices
        self.n_edges = 2 if self.n_slab > 2 else 1
        halves = (range(self.line // 2, self.line), range(self.line // 2))
        self.halves = [h for h in halves if len(h)]
        self.edge_counts = 2 * self.each
        self.edge_back = self.edge_counts + self.views * self.n_view * self.each
        self.edge_rows = self.edge_back + padded_16(self.views)
        self.bands = self.views * self.taps * self.band
        self.starts = self.bands + self.views * self.slices
        self.param_rows = self.starts + padded_16(2 * self.views * self.taps)
        self.first_counts = self.param_rows
        self.first_edges = self.first_counts + self.views * len(self.halves[0]) * self.block
        self.edges_each = self.views * self.line * self.each
        self.first_back = self.first_edges + self.n_edges * self.edges_each
        self.first_rows = self.first_back + self.n_edges * padded_16(self.views)

    def peer(self, at, k):
        xor = self.line & (self.line - 1) == 0
        return at ^ k if xor else (at + k) % self.line

    def across(self, k, towards):
        g = self.pairs
        moves = [(i, self.peer(i // g, k) * g + i % g) for i in range(self.n_view)]
        return moves if towards else [(j, i) for i, j in moves]

    def valid(self):
        slab = lax.axis_index("slab")
        return (slab > 0, slab < self.n_slab - 1)


def call(kernel, outs, *args, scratch=(), flops=0):
    size = lambda xs: sum(x.size * x.dtype.itemsize for x in xs)
    return pl.pallas_call(
        kernel,
        out_shape=outs,
        in_specs=[VMEM] * len(args),
        out_specs=[VMEM] * len(outs),
        scratch_shapes=list(scratch),
        compiler_params=pltpu.CompilerParams(vmem_limit_bytes=24 * 1024 * 1024),
        cost_estimate=pl.CostEstimate(
            flops=flops, bytes_accessed=size(args) + size(outs), transcendentals=0
        ),
    )(*args)


def valid_kernel(p, valid_ref):
    for high, valid in enumerate(p.valid()):
        valid_ref[high] = jnp.where(valid, jnp.ones((8, 128), F32), 0.0)


def pack_kernel(p, valid_ref, counts_ref, activity_ref, back_ref, edges_ref):
    lowest = valid_ref[0, 0:1, 0:1] == 0.0
    last = p.slices - 1
    activity = activity_ref[...].astype(F32)
    back = back_ref[...].astype(F32)
    for slot in range(p.n_edges):

        def edge(high, low):
            if p.n_edges == 2:
                return high if slot == 0 else low
            return jnp.where(lowest, high, low)

        for j in range(2):
            edges_ref[slot, j * p.each : (j + 1) * p.each] = edge(
                activity[:, last - 1 + j, :], activity[:, j, :]
            )
        for v in range(p.views):
            for r in range(p.n_view):
                at = p.edge_counts + (v * p.n_view + r) * p.each
                edges_ref[slot, at : at + p.each] = edge(
                    counts_ref[v, r, :, last, :], counts_ref[v, r, :, 0, :]
                ).astype(F32)
            edges_ref[slot, p.edge_back + v : p.edge_back + v + 1] = edge(
                back[v, last : last + 1], back[v, 0:1]
            )
        tail = p.edge_rows - p.edge_back - p.views
        if tail:
            edges_ref[slot, p.edge_back + p.views :] = jnp.zeros((tail, p.width), F32)


def send_kernel(p, edges_ref, counts_ref, activity_ref, back_ref, values_ref, starts_ref, payload_ref, *outs):
    at = lax.axis_index("view")
    at_line, side = at // p.pairs, at % p.pairs
    payload_ref[: p.block] = activity_ref[...].reshape(p.block, p.width)
    for e in range(p.n_edges):
        low = p.block + e * 2 * p.each
        payload_ref[low : low + 2 * p.each] = edges_ref[e, : 2 * p.each].astype(BF16)
    out = outs[0]
    for ks, later in zip(p.halves[1:], outs[1:]):
        copy_counts(p, ks, counts_ref, later, 0)
    out[: p.bands] = values_ref[...].reshape(p.bands, p.width)
    out[p.bands : p.starts] = back_ref[...].reshape(p.views * p.slices, p.width)
    starts = jnp.concatenate([starts_ref[t] for t in range(p.taps)], axis=0)
    pieces = [lax.shift_right_logical(starts, 7), starts & 127]
    tail = p.param_rows - p.starts - 2 * p.views * p.taps
    if tail:
        pieces.append(jnp.zeros((tail, p.width), I32))
    out[p.starts : p.param_rows] = jnp.concatenate(pieces, axis=0).astype(F32).astype(BF16)
    copy_counts(p, p.halves[0], counts_ref, out, p.first_counts)
    for e in range(p.n_edges):
        pieces = []
        for v in range(p.views):
            for k in range(p.line):
                row = p.peer(at_line, k) * 2 + (1 - side)
                start = p.edge_counts + (v * p.n_view + row) * p.each
                pieces.append(edges_ref[e, pl.ds(pl.multiple_of(start, p.each), p.each), :])
        low = p.first_edges + e * p.edges_each
        out[low : low + p.edges_each] = jnp.concatenate(pieces, axis=0).astype(BF16)
        low = p.first_back + e * padded_16(p.views)
        out[low : low + padded_16(p.views)] = edges_ref[
            e, p.edge_back : p.edge_back + padded_16(p.views)
        ].astype(BF16)


def copy_counts(p, ks, counts_ref, out, base):
    at = lax.axis_index("view")
    for v in range(p.views):
        for i, k in enumerate(ks):
            row = p.peer(at // p.pairs, k) * 2 + 1 - at % p.pairs
            low = base + (v * len(ks) + i) * p.block
            counts = counts_ref[v, row].astype(F32).astype(BF16)
            out[low : low + p.block] = counts.reshape(p.block, p.width)


def place_bands(values, start):
    width = values.shape[1]
    moved = jnp.concatenate([values, jnp.zeros((8, width), F32)], axis=0)
    for step in (1, 2, 4):
        moved = jnp.where((start & step) != 0, pltpu.roll(moved, step, 0), moved)
    step = 8
    while step < width:
        longer = min(moved.shape[0] + step, width)
        zeros = jnp.zeros((step, width), F32)
        down = jnp.concatenate([zeros, moved], axis=0)[:longer]
        stay = jnp.concatenate([moved, zeros], axis=0)[:longer]
        moved = jnp.where((start & step) != 0, down, stay)
        step *= 2
    return moved.astype(BF16)


def matrix_kernel(p, params_ref, matrix_ref):
    starts = params_ref[p.starts : p.param_rows].astype(F32).astype(I32)
    n = p.views * p.taps
    starts = starts[:n] * 128 + starts[n : 2 * n]
    for v in range(p.views):
        for t in range(p.taps):
            at = v * p.taps + t
            values = params_ref[at * p.band : (at + 1) * p.band].astype(F32)
            at = t * p.views + v
            matrix_ref[v, t] = place_bands(values, starts[at : at + 1])


def place_source(p, blocks, lifted_ref, source_ref):
    rows = len(blocks) * p.each
    for i, block_ref in enumerate(blocks):
        low = i * p.each
        lifted_ref[low : low + p.each, 8 : 8 + p.slices, :] = (
            block_ref[: p.block].astype(F32).reshape(p.each, p.slices, p.width)
        )
        edges = block_ref[p.block :].astype(F32)
        for high, valid in enumerate(p.valid()):
            for j in range(2):
                at = (2 * min(high, p.n_edges - 1) + j) * p.each
                lifted_ref[low : low + p.each, (8 + p.slices if high else 6) + j, :] = jnp.where(
                    valid, edges[at : at + p.each], 0.0
                )
    main = rows * p.slices
    for t in range(p.taps):
        source_ref[t, :main] = (
            lifted_ref[:, 7 + t : 7 + t + p.slices, :].astype(BF16).reshape(main, p.width)
        )
        source_ref[t, main:] = jnp.concatenate(
            [lifted_ref[:, 6 + t, :], lifted_ref[:, 7 + p.slices + t, :]], axis=0
        ).astype(BF16)


def rows_kernel(p, half, counts_ref, edges_ref, back_ref, matrix_ref, *refs):
    ks = p.halves[half]
    blocks, refs = refs[: len(ks)], refs[len(ks) :]
    refs = refs[half:]
    if p.pairs == 2:
        (their_ref, first_ref, their_matrix_ref), refs = refs[:3], refs[3:]
        base = p.first_counts if half == 0 else 0
    outs, (lifted_ref, source_ref, ratio_ref, up_ref, down_ref) = refs[: len(ks)], refs[len(ks) :]
    place_source(p, blocks, lifted_ref, source_ref)
    at = lax.axis_index("view")
    at_line, side = at // p.pairs, at % p.pairs
    rows = len(ks) * p.each
    main, full = rows * p.slices, rows * (p.slices + 2)
    views = []

    def view(matrix_ref, v, counts, back, edges, edge_backs):
        expected = None
        for t in range(p.taps):
            term = jnp.dot(source_ref[t], matrix_ref[v, t], preferred_element_type=F32)
            expected = term if expected is None else expected + term
        inner = expected[:main].reshape(rows, p.slices, p.width) + back[None]
        ratio = counts / inner - 1.0
        n = len(views)
        ratio_ref[n, :main] = ratio.astype(BF16).reshape(main, p.width)
        for high, valid in enumerate(p.valid()):
            low = main + high * rows
            e = min(high, p.n_edges - 1)
            ratio = edges[e] / (expected[low : low + rows] + edge_backs[e]) - 1.0
            ratio_ref[n, low : low + rows] = jnp.where(valid, ratio, 0.0).astype(BF16)
        views.append((matrix_ref, v))

    for v in range(p.views):
        counts, edges, edge_backs = [], [], []
        for k in ks:
            counts.append(counts_ref[v, p.peer(at_line, k) * p.pairs + side])
        for e in range(p.n_edges):
            pieces = []
            for k in ks:
                row = p.peer(at_line, k) * p.pairs + side
                start = p.edge_counts + (v * p.n_view + row) * p.each
                pieces.append(edges_ref[e, pl.ds(pl.multiple_of(start, p.each), p.each), :])
            edges.append(jnp.concatenate(pieces, axis=0))
            edge_backs.append(edges_ref[e, p.edge_back + v : p.edge_back + v + 1])
        counts = jnp.concatenate(counts, axis=0).astype(F32)
        view(matrix_ref, v, counts, back_ref[v].astype(F32), edges, edge_backs)
    if p.pairs == 2:
        for v in range(p.views):
            edges, edge_backs = [], []
            for e in range(p.n_edges):
                start = p.first_edges + e * p.edges_each + (v * p.line + ks[0]) * p.each
                edges.append(first_ref[start : start + rows].astype(F32))
                start = p.first_back + e * padded_16(p.views)
                backs = first_ref[start : start + padded_16(p.views)].astype(F32)
                edge_backs.append(backs[v : v + 1])
            counts = their_ref[base + v * main : base + (v + 1) * main].astype(F32)
            back = first_ref[p.bands + v * p.slices : p.bands + (v + 1) * p.slices].astype(F32)
            view(
                their_matrix_ref,
                v,
                counts.reshape(rows, p.slices, p.width),
                back,
                edges,
                edge_backs,
            )

    def project(tap, stop):
        total = None
        for n, (matrix_ref, v) in enumerate(views):
            term = lax.dot_general(
                ratio_ref[n, :stop],
                matrix_ref[v, tap],
                (((1,), (1,)), ((), ())),
                preferred_element_type=F32,
            )
            total = term if total is None else total + term
        return total

    part = project(0, full)
    up_ref[:, : p.slices, :] = part[:main].reshape(rows, p.slices, p.width)
    up_ref[:, p.slices, :] = part[main + rows :]
    part = project(2, main + rows)
    down_ref[:, 8 : 8 + p.slices, :] = part[:main].reshape(rows, p.slices, p.width)
    down_ref[:, 7, :] = part[main:]
    total = project(1, main).reshape(rows, p.slices, p.width)
    total = total + up_ref[:, 1 : 1 + p.slices, :] + down_ref[:, 7 : 7 + p.slices, :]
    for i, out in enumerate(outs):
        part = total[i * p.each : (i + 1) * p.each]
        out[...] = part


def sum_kernel(p, *refs):
    total = None
    for ref in refs[:-1]:
        total = ref[...] if total is None else total + ref[...]
    refs[-1][...] = total


def per_device(activity, histo_counts, background, blur_values, band_start):
    p = Plan(activity, histo_counts, blur_values)
    shape = jax.ShapeDtypeStruct
    part = lambda kernel, *static: functools.partial(kernel, p, *static)
    width = p.width
    other = [(i, i ^ 1) for i in range(p.n_view)]

    counts = histo_counts.reshape(p.views, p.n_view, p.each, p.slices, width)
    values = jnp.swapaxes(blur_values, 2, 3)
    starts = jnp.swapaxes(band_start, 0, 1)
    (valid,) = call(part(valid_kernel), [shape((2, 8, 128), F32)], flops=2 * 10**9)
    (edges,) = call(
        part(pack_kernel),
        [shape((p.n_edges, p.edge_rows, width), F32)],
        valid, counts, activity, background,
    )
    if p.n_slab == 2:
        edges = lax.ppermute(edges, "slab", [(0, 1), (1, 0)])
    elif p.n_slab > 2:
        up = [(i, i + 1) for i in range(p.n_slab - 1)]
        down = [(j, i) for i, j in up]
        edges = jnp.stack([lax.ppermute(edges[0], "slab", up), lax.ppermute(edges[1], "slab", down)])
    outs = [shape((p.block + 2 * p.n_edges * p.each, width), BF16), shape((p.first_rows, width), BF16)]
    outs += [shape((p.views * len(h) * p.block, width), BF16) for h in p.halves[1:]]
    payload, *sent = call(
        part(send_kernel), outs, edges, counts, activity, background, values, starts
    )
    theirs = [lax.ppermute(x, "view", other) for x in sent] if p.pairs == 2 else []
    far_first = range(p.line - 1, 0, -1)
    blocks = {k: lax.ppermute(payload, "view", p.across(k, False)) for k in far_first}
    blocks = [payload] + [blocks[k] for k in range(1, p.line)]

    matrices = shape((p.views, p.taps, width, width), BF16)
    (matrix,) = call(part(matrix_kernel), [matrices], sent[0])
    if p.pairs == 2:
        (their_matrix,) = call(part(matrix_kernel), [matrices], theirs[0])

    terms = {}
    for half, ks in enumerate(p.halves):
        args = [counts, edges, background, matrix] + [blocks[k] for k in ks]
        args += list(terms.values())[:half]
        if p.pairs == 2:
            args += [theirs[half], theirs[0], their_matrix]
        rows = len(ks) * p.each
        full = rows * (p.slices + 2)
        n_views = p.views * p.pairs
        plain = shape((p.each, p.slices, width), F32)
        outs = call(
            part(rows_kernel, half),
            [plain] * len(ks),
            *args,
            scratch=[
                pltpu.VMEM((rows, p.slices + 16, width), F32),
                pltpu.VMEM((p.taps, full, width), BF16),
                pltpu.VMEM((n_views, full, width), BF16),
                pltpu.VMEM((rows, p.slices + 8, width), F32),
                pltpu.VMEM((rows, p.slices + 8, width), F32),
            ],
            flops=4 * n_views * p.taps * full * width * width,
        )
        terms.update(zip(ks, outs))
    total = [terms[0]]
    for ks in p.halves:
        came = [lax.ppermute(terms[k], "view", p.across(k, True)) for k in ks if k]
        if came or ks[0] == 0:
            plain_terms = total if ks[0] == 0 else []
            done = call(part(sum_kernel), [plain], *came, *plain_terms)
            total = list(done) if ks[0] == 0 else total + list(done)
    return total[0]


def solution(mesh):
    placed = (
        P(("parts", "view"), "slab", None),
        P(("parts", "view"), None, "slab", None),
        P(("parts", "view"), "slab", None),
        P("view", None, None, None),
        P("view", None, None),
    )
    return jax.shard_map(
        per_device,
        mesh=mesh,
        in_specs=placed,
        out_specs=P(("parts", "view"), "slab", None),
        check_vma=False,
    )
```

```python
import functools

import jax
import jax.numpy as jnp
from jax import lax
from jax.experimental import pallas as pl
from jax.experimental.pallas import tpu as pltpu
from jax.sharding import PartitionSpec as P

VMEM = pl.BlockSpec(memory_space=pltpu.VMEM)
BF16, F32, I16, I32 = jnp.bfloat16, jnp.float32, jnp.int16, jnp.int32
FULL, STEPS = 32700.0, 64.0


def padded_16(rows):
    return -(-rows // 16) * 16


class Plan:
    def __init__(self, activity, histo_counts, blur_values):
        self.each, self.slices, self.width = activity.shape
        self.views, self.taps, _, self.band = blur_values.shape
        self.n_slab = lax.axis_size("slab")
        self.n_view = lax.axis_size("view")
        self.pairs = 2 if self.n_view % 2 == 0 else 1
        self.line = self.n_view // self.pairs
        self.block = self.each * self.slices
        self.n_edges = 2 if self.n_slab > 2 else 1
        halves = (range(self.line // 2, self.line), range(self.line // 2))
        self.halves = [h for h in halves if len(h)]
        self.edge_counts = 2 * self.each
        self.edge_back = self.edge_counts + self.views * self.n_view * self.each
        self.edge_rows = self.edge_back + padded_16(self.views)
        self.bands = self.views * self.taps * self.band
        self.starts = self.bands + self.views * self.slices
        self.param_rows = self.starts + padded_16(2 * self.views * self.taps)
        self.first_counts = self.param_rows
        self.first_edges = self.first_counts + self.views * len(self.halves[0]) * self.block
        self.edges_each = self.views * self.line * self.each
        self.first_back = self.first_edges + self.n_edges * self.edges_each
        self.first_rows = self.first_back + self.n_edges * padded_16(self.views)

    def peer(self, at, k):
        xor = self.line & (self.line - 1) == 0
        return at ^ k if xor else (at + k) % self.line

    def across(self, k, towards):
        g = self.pairs
        moves = [(i, self.peer(i // g, k) * g + i % g) for i in range(self.n_view)]
        return moves if towards else [(j, i) for i, j in moves]

    def valid(self):
        slab = lax.axis_index("slab")
        return (slab > 0, slab < self.n_slab - 1)


def call(kernel, outs, *args, scratch=(), flops=0):
    size = lambda xs: sum(x.size * x.dtype.itemsize for x in xs)
    return pl.pallas_call(
        kernel,
        out_shape=outs,
        in_specs=[VMEM] * len(args),
        out_specs=[VMEM] * len(outs),
        scratch_shapes=list(scratch),
        compiler_params=pltpu.CompilerParams(vmem_limit_bytes=24 * 1024 * 1024),
        cost_estimate=pl.CostEstimate(
            flops=flops, bytes_accessed=size(args) + size(outs), transcendentals=0
        ),
    )(*args)


def valid_kernel(p, valid_ref):
    for high, valid in enumerate(p.valid()):
        valid_ref[high] = jnp.where(valid, jnp.ones((8, 128), F32), 0.0)


def pack_kernel(p, valid_ref, counts_ref, activity_ref, back_ref, edges_ref):
    lowest = valid_ref[0, 0:1, 0:1] == 0.0
    last = p.slices - 1
    activity = activity_ref[...].astype(F32)
    back = back_ref[...].astype(F32)
    for slot in range(p.n_edges):

        def edge(high, low):
            if p.n_edges == 2:
                return high if slot == 0 else low
            return jnp.where(lowest, high, low)

        for j in range(2):
            edges_ref[slot, j * p.each : (j + 1) * p.each] = edge(
                activity[:, last - 1 + j, :], activity[:, j, :]
            )
        for v in range(p.views):
            for r in range(p.n_view):
                at = p.edge_counts + (v * p.n_view + r) * p.each
                edges_ref[slot, at : at + p.each] = edge(
                    counts_ref[v, r, :, last, :], counts_ref[v, r, :, 0, :]
                ).astype(F32)
            edges_ref[slot, p.edge_back + v : p.edge_back + v + 1] = edge(
                back[v, last : last + 1], back[v, 0:1]
            )
        tail = p.edge_rows - p.edge_back - p.views
        if tail:
            edges_ref[slot, p.edge_back + p.views :] = jnp.zeros((tail, p.width), F32)


def send_kernel(p, edges_ref, counts_ref, activity_ref, back_ref, values_ref, starts_ref, payload_ref, *outs):
    at = lax.axis_index("view")
    at_line, side = at // p.pairs, at % p.pairs
    payload_ref[: p.block] = activity_ref[...].reshape(p.block, p.width)
    for e in range(p.n_edges):
        low = p.block + e * 2 * p.each
        payload_ref[low : low + 2 * p.each] = edges_ref[e, : 2 * p.each].astype(BF16)
    out = outs[0]
    for ks, later in zip(p.halves[1:], outs[1:]):
        copy_counts(p, ks, counts_ref, later, 0)
    out[: p.bands] = values_ref[...].reshape(p.bands, p.width)
    out[p.bands : p.starts] = back_ref[...].reshape(p.views * p.slices, p.width)
    starts = jnp.concatenate([starts_ref[t] for t in range(p.taps)], axis=0)
    pieces = [lax.shift_right_logical(starts, 7), starts & 127]
    tail = p.param_rows - p.starts - 2 * p.views * p.taps
    if tail:
        pieces.append(jnp.zeros((tail, p.width), I32))
    out[p.starts : p.param_rows] = jnp.concatenate(pieces, axis=0).astype(F32).astype(BF16)
    copy_counts(p, p.halves[0], counts_ref, out, p.first_counts)
    for e in range(p.n_edges):
        pieces = []
        for v in range(p.views):
            for k in range(p.line):
                row = p.peer(at_line, k) * 2 + (1 - side)
                start = p.edge_counts + (v * p.n_view + row) * p.each
                pieces.append(edges_ref[e, pl.ds(pl.multiple_of(start, p.each), p.each), :])
        low = p.first_edges + e * p.edges_each
        out[low : low + p.edges_each] = jnp.concatenate(pieces, axis=0).astype(BF16)
        low = p.first_back + e * padded_16(p.views)
        out[low : low + padded_16(p.views)] = edges_ref[
            e, p.edge_back : p.edge_back + padded_16(p.views)
        ].astype(BF16)


def copy_counts(p, ks, counts_ref, out, base):
    at = lax.axis_index("view")
    for v in range(p.views):
        for i, k in enumerate(ks):
            row = p.peer(at // p.pairs, k) * 2 + 1 - at % p.pairs
            low = base + (v * len(ks) + i) * p.block
            counts = counts_ref[v, row].astype(F32).astype(BF16)
            out[low : low + p.block] = counts.reshape(p.block, p.width)


def place_bands(values, start):
    width = values.shape[1]
    moved = jnp.concatenate([values, jnp.zeros((8, width), F32)], axis=0)
    for step in (1, 2, 4):
        moved = jnp.where((start & step) != 0, pltpu.roll(moved, step, 0), moved)
    step = 8
    while step < width:
        longer = min(moved.shape[0] + step, width)
        zeros = jnp.zeros((step, width), F32)
        down = jnp.concatenate([zeros, moved], axis=0)[:longer]
        stay = jnp.concatenate([moved, zeros], axis=0)[:longer]
        moved = jnp.where((start & step) != 0, down, stay)
        step *= 2
    return moved.astype(BF16)


def matrix_kernel(p, params_ref, matrix_ref):
    starts = params_ref[p.starts : p.param_rows].astype(F32).astype(I32)
    n = p.views * p.taps
    starts = starts[:n] * 128 + starts[n : 2 * n]
    for v in range(p.views):
        for t in range(p.taps):
            at = v * p.taps + t
            values = params_ref[at * p.band : (at + 1) * p.band].astype(F32)
            at = t * p.views + v
            matrix_ref[v, t] = place_bands(values, starts[at : at + 1])


def place_source(p, blocks, lifted_ref, source_ref):
    rows = len(blocks) * p.each
    for i, block_ref in enumerate(blocks):
        low = i * p.each
        lifted_ref[low : low + p.each, 8 : 8 + p.slices, :] = (
            block_ref[: p.block].astype(F32).reshape(p.each, p.slices, p.width)
        )
        edges = block_ref[p.block :].astype(F32)
        for high, valid in enumerate(p.valid()):
            for j in range(2):
                at = (2 * min(high, p.n_edges - 1) + j) * p.each
                lifted_ref[low : low + p.each, (8 + p.slices if high else 6) + j, :] = jnp.where(
                    valid, edges[at : at + p.each], 0.0
                )
    main = rows * p.slices
    for t in range(p.taps):
        source_ref[t, :main] = (
            lifted_ref[:, 7 + t : 7 + t + p.slices, :].astype(BF16).reshape(main, p.width)
        )
        source_ref[t, main:] = jnp.concatenate(
            [lifted_ref[:, 6 + t, :], lifted_ref[:, 7 + p.slices + t, :]], axis=0
        ).astype(BF16)


def rows_kernel(p, half, counts_ref, edges_ref, back_ref, matrix_ref, *refs):
    ks = p.halves[half]
    blocks, refs = refs[: len(ks)], refs[len(ks) :]
    refs = refs[half:]
    if p.pairs == 2:
        (their_ref, first_ref, their_matrix_ref), refs = refs[:3], refs[3:]
        base = p.first_counts if half == 0 else 0
    outs, (lifted_ref, source_ref, ratio_ref, up_ref, down_ref) = refs[: len(ks)], refs[len(ks) :]
    place_source(p, blocks, lifted_ref, source_ref)
    at = lax.axis_index("view")
    at_line, side = at // p.pairs, at % p.pairs
    rows = len(ks) * p.each
    main, full = rows * p.slices, rows * (p.slices + 2)
    views = []

    def view(matrix_ref, v, counts, back, edges, edge_backs):
        expected = None
        for t in range(p.taps):
            term = jnp.dot(source_ref[t], matrix_ref[v, t], preferred_element_type=F32)
            expected = term if expected is None else expected + term
        inner = expected[:main].reshape(rows, p.slices, p.width) + back[None]
        ratio = counts / inner - 1.0
        n = len(views)
        ratio_ref[n, :main] = ratio.astype(BF16).reshape(main, p.width)
        for high, valid in enumerate(p.valid()):
            low = main + high * rows
            e = min(high, p.n_edges - 1)
            ratio = edges[e] / (expected[low : low + rows] + edge_backs[e]) - 1.0
            ratio_ref[n, low : low + rows] = jnp.where(valid, ratio, 0.0).astype(BF16)
        views.append((matrix_ref, v))

    for v in range(p.views):
        counts, edges, edge_backs = [], [], []
        for k in ks:
            counts.append(counts_ref[v, p.peer(at_line, k) * p.pairs + side])
        for e in range(p.n_edges):
            pieces = []
            for k in ks:
                row = p.peer(at_line, k) * p.pairs + side
                start = p.edge_counts + (v * p.n_view + row) * p.each
                pieces.append(edges_ref[e, pl.ds(pl.multiple_of(start, p.each), p.each), :])
            edges.append(jnp.concatenate(pieces, axis=0))
            edge_backs.append(edges_ref[e, p.edge_back + v : p.edge_back + v + 1])
        counts = jnp.concatenate(counts, axis=0).astype(F32)
        view(matrix_ref, v, counts, back_ref[v].astype(F32), edges, edge_backs)
    if p.pairs == 2:
        for v in range(p.views):
            edges, edge_backs = [], []
            for e in range(p.n_edges):
                start = p.first_edges + e * p.edges_each + (v * p.line + ks[0]) * p.each
                edges.append(first_ref[start : start + rows].astype(F32))
                start = p.first_back + e * padded_16(p.views)
                backs = first_ref[start : start + padded_16(p.views)].astype(F32)
                edge_backs.append(backs[v : v + 1])
            counts = their_ref[base + v * main : base + (v + 1) * main].astype(F32)
            back = first_ref[p.bands + v * p.slices : p.bands + (v + 1) * p.slices].astype(F32)
            view(
                their_matrix_ref,
                v,
                counts.reshape(rows, p.slices, p.width),
                back,
                edges,
                edge_backs,
            )

    def project(tap, stop):
        total = None
        for n, (matrix_ref, v) in enumerate(views):
            term = lax.dot_general(
                ratio_ref[n, :stop],
                matrix_ref[v, tap],
                (((1,), (1,)), ((), ())),
                preferred_element_type=F32,
            )
            total = term if total is None else total + term
        return total

    part = project(0, full)
    up_ref[:, : p.slices, :] = part[:main].reshape(rows, p.slices, p.width)
    up_ref[:, p.slices, :] = part[main + rows :]
    part = project(2, main + rows)
    down_ref[:, 8 : 8 + p.slices, :] = part[:main].reshape(rows, p.slices, p.width)
    down_ref[:, 7, :] = part[main:]
    total = project(1, main).reshape(rows, p.slices, p.width)
    total = total + up_ref[:, 1 : 1 + p.slices, :] + down_ref[:, 7 : 7 + p.slices, :]
    for i, out in enumerate(outs):
        part = total[i * p.each : (i + 1) * p.each]
        if ks[i] == 0:
            out[...] = part
        else:
            encode(p, part, out)


def encode(p, x, out_ref):
    most = jnp.maximum(jnp.max(jnp.abs(x), axis=1), 1e-30)
    power = jnp.ceil(jnp.log2(most) * STEPS)
    codes = jnp.round(x * (FULL * jnp.exp2(power * (-1.0 / STEPS)))[:, None, :])
    out_ref[: p.block] = codes.reshape(p.block, p.width).astype(I32).astype(I16)
    tail = padded_16(p.each) - p.each
    if tail:
        power = jnp.concatenate([power, jnp.zeros((tail, p.width), F32)], axis=0)
    out_ref[p.block :] = power.astype(I32).astype(I16)


def decode(p, in_ref):
    power = in_ref[p.block :].astype(I32).astype(F32)[: p.each]
    scale = jnp.exp2(power * (1.0 / STEPS)) * (1.0 / FULL)
    codes = in_ref[: p.block].astype(I32).astype(F32)
    return codes.reshape(p.each, p.slices, p.width) * scale[:, None, :]


def sum_kernel(p, coded, *refs):
    total = None
    for i, ref in enumerate(refs[:-1]):
        term = decode(p, ref) if i < coded else ref[...]
        total = term if total is None else total + term
    refs[-1][...] = total


def per_device(activity, histo_counts, background, blur_values, band_start):
    p = Plan(activity, histo_counts, blur_values)
    shape = jax.ShapeDtypeStruct
    part = lambda kernel, *static: functools.partial(kernel, p, *static)
    width = p.width
    other = [(i, i ^ 1) for i in range(p.n_view)]

    counts = histo_counts.reshape(p.views, p.n_view, p.each, p.slices, width)
    values = jnp.swapaxes(blur_values, 2, 3)
    starts = jnp.swapaxes(band_start, 0, 1)
    (valid,) = call(part(valid_kernel), [shape((2, 8, 128), F32)], flops=2 * 10**9)
    (edges,) = call(
        part(pack_kernel),
        [shape((p.n_edges, p.edge_rows, width), F32)],
        valid, counts, activity, background,
    )
    if p.n_slab == 2:
        edges = lax.ppermute(edges, "slab", [(0, 1), (1, 0)])
    elif p.n_slab > 2:
        up = [(i, i + 1) for i in range(p.n_slab - 1)]
        down = [(j, i) for i, j in up]
        edges = jnp.stack([lax.ppermute(edges[0], "slab", up), lax.ppermute(edges[1], "slab", down)])
    outs = [shape((p.block + 2 * p.n_edges * p.each, width), BF16), shape((p.first_rows, width), BF16)]
    outs += [shape((p.views * len(h) * p.block, width), BF16) for h in p.halves[1:]]
    payload, *sent = call(
        part(send_kernel), outs, edges, counts, activity, background, values, starts
    )
    theirs = [lax.ppermute(x, "view", other) for x in sent] if p.pairs == 2 else []
    far_first = range(p.line - 1, 0, -1)
    blocks = {k: lax.ppermute(payload, "view", p.across(k, False)) for k in far_first}
    blocks = [payload] + [blocks[k] for k in range(1, p.line)]

    matrices = shape((p.views, p.taps, width, width), BF16)
    (matrix,) = call(part(matrix_kernel), [matrices], sent[0])
    if p.pairs == 2:
        (their_matrix,) = call(part(matrix_kernel), [matrices], theirs[0])

    terms = {}
    for half, ks in enumerate(p.halves):
        args = [counts, edges, background, matrix] + [blocks[k] for k in ks]
        args += list(terms.values())[:half]
        if p.pairs == 2:
            args += [theirs[half], theirs[0], their_matrix]
        rows = len(ks) * p.each
        full = rows * (p.slices + 2)
        n_views = p.views * p.pairs
        code = shape((p.block + padded_16(p.each), width), I16)
        plain = shape((p.each, p.slices, width), F32)
        outs = call(
            part(rows_kernel, half),
            [code if k else plain for k in ks],
            *args,
            scratch=[
                pltpu.VMEM((rows, p.slices + 16, width), F32),
                pltpu.VMEM((p.taps, full, width), BF16),
                pltpu.VMEM((n_views, full, width), BF16),
                pltpu.VMEM((rows, p.slices + 8, width), F32),
                pltpu.VMEM((rows, p.slices + 8, width), F32),
            ],
            flops=4 * n_views * p.taps * full * width * width,
        )
        terms.update(zip(ks, outs))
    total = [terms[0]]
    for ks in p.halves:
        came = [lax.ppermute(terms[k], "view", p.across(k, True)) for k in ks if k]
        if came or ks[0] == 0:
            plain_terms = total if ks[0] == 0 else []
            done = call(part(sum_kernel, len(came)), [plain], *came, *plain_terms)
            total = list(done) if ks[0] == 0 else total + list(done)
    return total[0]


def solution(mesh):
    placed = (
        P(("parts", "view"), "slab", None),
        P(("parts", "view"), None, "slab", None),
        P(("parts", "view"), "slab", None),
        P("view", None, None, None),
        P("view", None, None),
    )
    return jax.shard_map(
        per_device,
        mesh=mesh,
        in_specs=placed,
        out_specs=P(("parts", "view"), "slab", None),
        check_vma=False,
    )
```

```python
import functools

import jax
import jax.numpy as jnp
from jax import lax
from jax.experimental import pallas as pl
from jax.experimental.pallas import tpu as pltpu
from jax.sharding import PartitionSpec as P

VMEM = pl.BlockSpec(memory_space=pltpu.VMEM)
BF16, F32, I16, I32 = jnp.bfloat16, jnp.float32, jnp.int16, jnp.int32
FULL, STEPS = 32700.0, 64.0


def padded_16(rows):
    return -(-rows // 16) * 16


class Plan:
    def __init__(self, activity, histo_counts, blur_values):
        self.each, self.slices, self.width = activity.shape
        self.views, self.taps, _, self.band = blur_values.shape
        self.n_slab = lax.axis_size("slab")
        self.n_view = lax.axis_size("view")
        self.pairs = 2 if self.n_view % 2 == 0 else 1
        self.line = self.n_view // self.pairs
        self.block = self.each * self.slices
        self.n_edges = 2 if self.n_slab > 2 else 1
        half = self.line // 2
        stages = [s for s in (range(half, self.line), range(1, half), range(1)) if len(s)]
        self.stages = [list(s) for s in stages] if half else [[0]]
        self.messages = [[0], list(range(1, len(self.stages)))][: len(self.stages)]
        self.edge_counts = 2 * self.each
        self.edge_back = self.edge_counts + self.views * self.n_view * self.each
        self.edge_rows = self.edge_back + padded_16(self.views)
        self.bands = self.views * self.taps * self.band
        self.starts = self.bands + self.views * self.slices
        self.edge_backs = self.starts + 2 * self.views * self.taps
        need = self.edge_backs + self.n_edges * self.views
        self.param_rows = self.starts + padded_16(need - self.starts)

    def message_peers(self, m):
        return [k for s in self.messages[m] for k in self.stages[s]]

    def base(self, m):
        return 0 if m else self.param_rows

    def message_edges(self, m):
        return self.base(m) + self.views * len(self.message_peers(m)) * self.block

    def edges_each(self, m):
        return padded_16(self.views * len(self.message_peers(m)) * self.each)

    def message_rows(self, m):
        return self.message_edges(m) + self.n_edges * self.edges_each(m)

    def peer(self, at, k):
        xor = self.line & (self.line - 1) == 0
        return at ^ k if xor else (at + k) % self.line

    def across(self, k, towards):
        g = self.pairs
        moves = [(i, self.peer(i // g, k) * g + i % g) for i in range(self.n_view)]
        return moves if towards else [(j, i) for i, j in moves]

    def valid(self):
        slab = lax.axis_index("slab")
        return (slab > 0, slab < self.n_slab - 1)


def call(kernel, outs, *args, scratch=(), flops=0):
    size = lambda xs: sum(x.size * x.dtype.itemsize for x in xs)
    return pl.pallas_call(
        kernel,
        out_shape=outs,
        in_specs=[VMEM] * len(args),
        out_specs=[VMEM] * len(outs),
        scratch_shapes=list(scratch),
        compiler_params=pltpu.CompilerParams(vmem_limit_bytes=24 * 1024 * 1024),
        cost_estimate=pl.CostEstimate(
            flops=flops, bytes_accessed=size(args) + size(outs), transcendentals=0
        ),
    )(*args)


def valid_kernel(p, valid_ref):
    for high, valid in enumerate(p.valid()):
        valid_ref[high] = jnp.where(valid, jnp.ones((8, 128), F32), 0.0)


def pack_kernel(p, valid_ref, counts_ref, activity_ref, back_ref, edges_ref):
    lowest = valid_ref[0, 0:1, 0:1] == 0.0
    last = p.slices - 1
    activity = activity_ref[...].astype(F32)
    back = back_ref[...].astype(F32)
    for slot in range(p.n_edges):

        def edge(high, low):
            if p.n_edges == 2:
                return high if slot == 0 else low
            return jnp.where(lowest, high, low)

        for j in range(2):
            edges_ref[slot, j * p.each : (j + 1) * p.each] = edge(
                activity[:, last - 1 + j, :], activity[:, j, :]
            )
        for v in range(p.views):
            for r in range(p.n_view):
                at = p.edge_counts + (v * p.n_view + r) * p.each
                edges_ref[slot, at : at + p.each] = edge(
                    counts_ref[v, r, :, last, :], counts_ref[v, r, :, 0, :]
                ).astype(F32)
            edges_ref[slot, p.edge_back + v : p.edge_back + v + 1] = edge(
                back[v, last : last + 1], back[v, 0:1]
            )
        tail = p.edge_rows - p.edge_back - p.views
        if tail:
            edges_ref[slot, p.edge_back + p.views :] = jnp.zeros((tail, p.width), F32)


def send_kernel(p, edges_ref, counts_ref, activity_ref, back_ref, values_ref, starts_ref, payload_ref, *outs):
    payload_ref[: p.block] = activity_ref[...].reshape(p.block, p.width)
    for e in range(p.n_edges):
        low = p.block + e * 2 * p.each
        payload_ref[low : low + 2 * p.each] = edges_ref[e, : 2 * p.each].astype(BF16)
    out = outs[0]
    out[: p.bands] = values_ref[...].reshape(p.bands, p.width)
    out[p.bands : p.starts] = back_ref[...].reshape(p.views * p.slices, p.width)
    starts = jnp.concatenate([starts_ref[t] for t in range(p.taps)], axis=0)
    pieces = [lax.shift_right_logical(starts, 7).astype(F32), (starts & 127).astype(F32)]
    pieces += [edges_ref[e, p.edge_back : p.edge_back + p.views] for e in range(p.n_edges)]
    tail = p.param_rows - p.edge_backs - p.n_edges * p.views
    if tail:
        pieces.append(jnp.zeros((tail, p.width), F32))
    out[p.starts : p.param_rows] = jnp.concatenate(pieces, axis=0).astype(BF16)
    for m, out in enumerate(outs):
        put_counts(p, m, edges_ref, counts_ref, out)


def put_counts(p, m, edges_ref, counts_ref, out):
    at = lax.axis_index("view")
    ks = p.message_peers(m)
    rows = [p.peer(at // p.pairs, k) * p.pairs + p.pairs - 1 - at % p.pairs for k in ks]
    for v in range(p.views):
        for i, row in enumerate(rows):
            low = p.base(m) + (v * len(ks) + i) * p.block
            counts = counts_ref[v, row].astype(F32).astype(BF16)
            out[low : low + p.block] = counts.reshape(p.block, p.width)
    for e in range(p.n_edges):
        pieces = []
        for v in range(p.views):
            for row in rows:
                start = p.edge_counts + (v * p.n_view + row) * p.each
                pieces.append(edges_ref[e, pl.ds(pl.multiple_of(start, p.each), p.each), :])
        tail = p.edges_each(m) - len(pieces) * p.each
        if tail:
            pieces.append(jnp.zeros((tail, p.width), F32))
        low = p.message_edges(m) + e * p.edges_each(m)
        out[low : low + p.edges_each(m)] = jnp.concatenate(pieces, axis=0).astype(BF16)


def place_bands(values, start):
    width = values.shape[1]
    moved = jnp.concatenate([values, jnp.zeros((8, width), F32)], axis=0)
    for step in (1, 2, 4):
        moved = jnp.where((start & step) != 0, pltpu.roll(moved, step, 0), moved)
    step = 8
    while step < width:
        longer = min(moved.shape[0] + step, width)
        zeros = jnp.zeros((step, width), F32)
        down = jnp.concatenate([zeros, moved], axis=0)[:longer]
        stay = jnp.concatenate([moved, zeros], axis=0)[:longer]
        moved = jnp.where((start & step) != 0, down, stay)
        step *= 2
    return moved.astype(BF16)


def matrix_kernel(p, params_ref, *refs):
    matrix_ref = refs[-1]
    starts = params_ref[p.starts : p.param_rows].astype(F32).astype(I32)
    n = p.views * p.taps
    starts = starts[:n] * 128 + starts[n : 2 * n]
    for v in range(p.views):
        for t in range(p.taps):
            at = v * p.taps + t
            values = params_ref[at * p.band : (at + 1) * p.band].astype(F32)
            at = t * p.views + v
            matrix_ref[v, t] = place_bands(values, starts[at : at + 1])


def place_source(p, blocks, lifted_ref, source_ref):
    rows = len(blocks) * p.each
    for i, block_ref in enumerate(blocks):
        low = i * p.each
        lifted_ref[low : low + p.each, 8 : 8 + p.slices, :] = (
            block_ref[: p.block].astype(F32).reshape(p.each, p.slices, p.width)
        )
        edges = block_ref[p.block :].astype(F32)
        for high, valid in enumerate(p.valid()):
            for j in range(2):
                at = (2 * min(high, p.n_edges - 1) + j) * p.each
                lifted_ref[low : low + p.each, (8 + p.slices if high else 6) + j, :] = jnp.where(
                    valid, edges[at : at + p.each], 0.0
                )
    main = rows * p.slices
    for t in range(p.taps):
        source_ref[t, :main] = (
            lifted_ref[:, 7 + t : 7 + t + p.slices, :].astype(BF16).reshape(main, p.width)
        )
        source_ref[t, main:] = jnp.concatenate(
            [lifted_ref[:, 6 + t, :], lifted_ref[:, 7 + p.slices + t, :]], axis=0
        ).astype(BF16)


class Rows:
    def __init__(self, p, stage, source_ref, ratio_ref, up_ref, down_ref):
        self.p, self.source_ref, self.ratio_ref, self.views = p, source_ref, ratio_ref, []
        self.up_ref, self.down_ref = up_ref, down_ref
        self.rows = len(p.stages[stage]) * p.each
        self.main, self.full = self.rows * p.slices, self.rows * (p.slices + 2)

    def view(self, matrix_ref, v, counts, back, edges, edge_backs):
        p, rows, main = self.p, self.rows, self.main
        expected = None
        for t in range(p.taps):
            term = jnp.dot(self.source_ref[t], matrix_ref[v, t], preferred_element_type=F32)
            expected = term if expected is None else expected + term
        inner = expected[:main].reshape(rows, p.slices, p.width) + back[None]
        ratio = counts.astype(F32).reshape(rows, p.slices, p.width) / inner - 1.0
        n = len(self.views)
        self.ratio_ref[n, :main] = ratio.astype(BF16).reshape(main, p.width)
        outer = []
        for high, valid in enumerate(p.valid()):
            low = main + high * rows
            e = min(high, p.n_edges - 1)
            ratio = edges[e] / (expected[low : low + rows] + edge_backs[e]) - 1.0
            outer.append(jnp.where(valid, ratio, 0.0))
        self.ratio_ref[n, main:] = jnp.concatenate(outer, axis=0).astype(BF16)
        self.views.append((matrix_ref, v))

    def project(self, tap, stop):
        total = None
        for n, (matrix_ref, v) in enumerate(self.views):
            term = lax.dot_general(
                self.ratio_ref[n, :stop],
                matrix_ref[v, tap],
                (((1,), (1,)), ((), ())),
                preferred_element_type=F32,
            )
            total = term if total is None else total + term
        return total

    def gradient(self):
        p, rows, main, full = self.p, self.rows, self.main, self.full
        shape = (rows, p.slices, p.width)
        part = self.project(0, full)
        self.up_ref[:, : p.slices, :] = part[:main].reshape(shape)
        self.up_ref[:, p.slices, :] = part[main + rows :]
        part = self.project(2, full)
        self.down_ref[:, 8 : 8 + p.slices, :] = part[:main].reshape(shape)
        self.down_ref[:, 7, :] = part[main : main + rows]
        total = self.project(1, main).reshape(shape)
        return total + self.up_ref[:, 1 : 1 + p.slices, :] + self.down_ref[:, 7 : 7 + p.slices, :]


def own_kernel(p, stage, counts_ref, edges_ref, back_ref, matrix_ref, *refs):
    ks = p.stages[stage]
    blocks, refs = refs[: len(ks)], refs[len(ks) :]
    refs = refs[min(stage, 1) :]
    source_ref, total_ref, lifted_ref, *scratch = refs
    place_source(p, blocks, lifted_ref, source_ref)
    work = Rows(p, stage, source_ref, *scratch)
    at = lax.axis_index("view")
    places = [p.peer(at // p.pairs, k) * p.pairs + at % p.pairs for k in ks]
    for v in range(p.views):
        edges, edge_backs = [], []
        for e in range(p.n_edges):
            pieces = []
            for row in places:
                start = p.edge_counts + (v * p.n_view + row) * p.each
                pieces.append(edges_ref[e, pl.ds(pl.multiple_of(start, p.each), p.each), :])
            edges.append(jnp.concatenate(pieces, axis=0))
            edge_backs.append(edges_ref[e, p.edge_back + v : p.edge_back + v + 1])
        counts = jnp.concatenate([counts_ref[v, row] for row in places], axis=0)
        work.view(matrix_ref, v, counts, back_ref[v].astype(F32), edges, edge_backs)
    total_ref[...] = work.gradient()


def their_kernel(p, stage, after, source_ref, total_ref, *refs):
    ks = p.stages[stage]
    refs = refs[after:]
    total = total_ref[...]
    if p.pairs == 2:
        (message_ref, first_ref, matrix_ref), refs = refs[:3], refs[3:]
    outs, scratch = refs[: len(ks)], refs[len(ks) :]
    if p.pairs == 2:
        work = Rows(p, stage, source_ref, *scratch)
        (m,) = [m for m, stages in enumerate(p.messages) if stage in stages]
        peers = p.message_peers(m)
        skip = peers.index(ks[0])
        last = first_ref[p.starts : p.param_rows].astype(F32)
        came = []
        for e in range(p.n_edges):
            low = p.message_edges(m) + e * p.edges_each(m)
            came.append(message_ref[low : low + p.edges_each(m)].astype(F32))
        for v in range(p.views):
            low = (v * len(peers) + skip) * p.each
            edges = [x[low : low + work.rows] for x in came]
            low = p.edge_backs - p.starts + v
            edge_backs = [
                last[low + e * p.views : low + e * p.views + 1] for e in range(p.n_edges)
            ]
            low = p.base(m) + (v * len(peers) + skip) * p.block
            back = first_ref[p.bands + v * p.slices : p.bands + (v + 1) * p.slices].astype(F32)
            counts = message_ref[low : low + work.main]
            work.view(matrix_ref, v, counts, back, edges, edge_backs)
        total = total + work.gradient()
    for i, out in enumerate(outs):
        part = total[i * p.each : (i + 1) * p.each]
        if ks[i] == 0:
            out[...] = part
        else:
            encode(p, part, out)


def encode(p, x, out_ref):
    most = jnp.maximum(jnp.max(jnp.abs(x), axis=1), 1e-30)
    power = jnp.ceil(jnp.log2(most) * STEPS)
    codes = jnp.round(x * (FULL * jnp.exp2(power * (-1.0 / STEPS)))[:, None, :])
    out_ref[: p.block] = codes.reshape(p.block, p.width).astype(I32).astype(I16)
    tail = padded_16(p.each) - p.each
    if tail:
        power = jnp.concatenate([power, jnp.zeros((tail, p.width), F32)], axis=0)
    out_ref[p.block :] = power.astype(I32).astype(I16)


def decode(p, in_ref):
    power = in_ref[p.block :].astype(I32).astype(F32)[: p.each]
    scale = jnp.exp2(power * (1.0 / STEPS)) * (1.0 / FULL)
    codes = in_ref[: p.block].astype(I32).astype(F32)
    return codes.reshape(p.each, p.slices, p.width) * scale[:, None, :]


def sum_kernel(p, coded, *refs):
    total = None
    for i, ref in enumerate(refs[:-1]):
        term = decode(p, ref) if i < coded else ref[...]
        total = term if total is None else total + term
    refs[-1][...] = total


def per_device(activity, histo_counts, background, blur_values, band_start):
    p = Plan(activity, histo_counts, blur_values)
    shape = jax.ShapeDtypeStruct
    part = lambda kernel, *static: functools.partial(kernel, p, *static)
    width = p.width
    other = [(i, i ^ 1) for i in range(p.n_view)]

    counts = histo_counts.reshape(p.views, p.n_view, p.each, p.slices, width)
    values = jnp.swapaxes(blur_values, 2, 3)
    starts = jnp.swapaxes(band_start, 0, 1)
    (valid,) = call(part(valid_kernel), [shape((2, 8, 128), F32)], flops=2 * 10**9)
    (edges,) = call(
        part(pack_kernel),
        [shape((p.n_edges, p.edge_rows, width), F32)],
        valid, counts, activity, background,
    )
    if p.n_slab == 2:
        edges = lax.ppermute(edges, "slab", [(0, 1), (1, 0)])
    elif p.n_slab > 2:
        up = [(i, i + 1) for i in range(p.n_slab - 1)]
        down = [(j, i) for i, j in up]
        edges = jnp.stack([lax.ppermute(edges[0], "slab", up), lax.ppermute(edges[1], "slab", down)])
    outs = [shape((p.block + 2 * p.n_edges * p.each, width), BF16)]
    outs += [shape((p.message_rows(m), width), BF16) for m in range(len(p.messages))]
    payload, *sent = call(
        part(send_kernel), outs, edges, counts, activity, background, values, starts
    )
    theirs = [lax.ppermute(x, "view", other) for x in sent] if p.pairs == 2 else []
    blocks = {0: payload}
    for k in [k for ks in p.stages for k in ks if k]:
        blocks[k] = lax.ppermute(payload, "view", p.across(k, False))

    matrices = shape((p.views, p.taps, width, width), BF16)
    (matrix,) = call(part(matrix_kernel), [matrices], sent[0])
    own = []
    for stage, ks in enumerate(p.stages):
        rows = len(ks) * p.each
        full = rows * (p.slices + 2)
        scratch = [
            pltpu.VMEM((p.views, full, width), BF16),
            pltpu.VMEM((rows, p.slices + 8, width), F32),
            pltpu.VMEM((rows, p.slices + 8, width), F32),
        ]
        own.append(
            call(
                part(own_kernel, stage),
                [
                    shape((p.taps, full, width), BF16),
                    shape((rows, p.slices, width), F32),
                ],
                counts, edges, background, matrix, *[blocks[k] for k in ks],
                *[blocks[p.stages[0][-1]]][: min(stage, 1)],
                scratch=[pltpu.VMEM((rows, p.slices + 16, width), F32)] + scratch,
                flops=4 * p.views * p.taps * full * width * width,
            )
        )
    if p.pairs == 2:
        (their_matrix,) = call(part(matrix_kernel), [matrices], theirs[0])

    code = shape((p.block + padded_16(p.each), width), I16)
    plain = shape((p.each, p.slices, width), F32)
    terms = {}
    for stage, ks in enumerate(p.stages):
        rows = len(ks) * p.each
        full = rows * (p.slices + 2)
        before = list(terms.values())[-1:]
        args = [*own[stage], *before]
        if p.pairs == 2:
            (m,) = [m for m, stages in enumerate(p.messages) if stage in stages]
            args += [theirs[m], theirs[0], their_matrix]
        outs = call(
            part(their_kernel, stage, len(before)),
            [code if k else plain for k in ks],
            *args,
            scratch=[
                pltpu.VMEM((p.views, full, width), BF16),
                pltpu.VMEM((rows, p.slices + 8, width), F32),
                pltpu.VMEM((rows, p.slices + 8, width), F32),
            ],
            flops=4 * p.views * p.taps * full * width * width,
        )
        terms.update(zip(ks, outs))
    total = []
    for m in range(len(p.messages)):
        came = [
            lax.ppermute(terms[k], "view", p.across(k, True)) for k in p.message_peers(m) if k
        ]
        if m == len(p.messages) - 1:
            total = total + [terms[0]]
        total = list(call(part(sum_kernel, len(came)), [plain], *came, *total))
    return total[0]


def solution(mesh):
    placed = (
        P(("parts", "view"), "slab", None),
        P(("parts", "view"), None, "slab", None),
        P(("parts", "view"), "slab", None),
        P("view", None, None, None),
        P("view", None, None),
    )
    return jax.shard_map(
        per_device,
        mesh=mesh,
        in_specs=placed,
        out_specs=P(("parts", "view"), "slab", None),
        check_vma=False,
    )
```

```python
import functools

import jax
import jax.numpy as jnp
from jax import lax
from jax.experimental import pallas as pl
from jax.experimental.pallas import tpu as pltpu
from jax.sharding import PartitionSpec as P

VMEM = pl.BlockSpec(memory_space=pltpu.VMEM)
BF16, F32, I16, I32 = jnp.bfloat16, jnp.float32, jnp.int16, jnp.int32
LONG = 8 * 10**9
FULL, STEPS = 32700.0, 64.0


def padded_16(rows):
    return -(-rows // 16) * 16


class Plan:
    def __init__(self, activity, histo_counts, blur_values):
        self.each, self.slices, self.width = activity.shape
        self.views, self.taps, _, self.band = blur_values.shape
        self.n_slab = lax.axis_size("slab")
        self.n_view = lax.axis_size("view")
        self.pairs = 2 if self.n_view % 2 == 0 else 1
        self.line = self.n_view // self.pairs
        self.block = self.each * self.slices
        self.n_edges = 2 if self.n_slab > 2 else 1
        half = self.line // 2
        stages = [s for s in (range(half, self.line), range(1, half), range(1)) if len(s)]
        self.stages = [list(s) for s in stages] if half else [[0]]
        self.messages = [[0], list(range(1, len(self.stages)))][: len(self.stages)]
        self.edge_counts = 2 * self.each
        self.edge_back = self.edge_counts + self.views * self.n_view * self.each
        self.edge_rows = self.edge_back + padded_16(self.views)
        self.bands = self.views * self.taps * self.band
        self.starts = self.bands + self.views * self.slices
        self.param_rows = self.starts + padded_16(2 * self.views * self.taps)
        self.order = [k for s in self.stages for k in s]
        self.early_back = self.views * self.line * self.each
        self.early_rows = padded_16(self.early_back + self.views)

    def message_peers(self, m):
        return [k for s in self.messages[m] for k in self.stages[s]]

    def base(self, m):
        return 0 if m else self.param_rows

    def message_rows(self, m):
        return self.base(m) + self.views * len(self.message_peers(m)) * self.block

    def peer(self, at, k):
        xor = self.line & (self.line - 1) == 0
        return at ^ k if xor else (at + k) % self.line

    def across(self, k, towards):
        g = self.pairs
        moves = [(i, self.peer(i // g, k) * g + i % g) for i in range(self.n_view)]
        return moves if towards else [(j, i) for i, j in moves]

    def valid(self):
        slab = lax.axis_index("slab")
        return (slab > 0, slab < self.n_slab - 1)


def call(kernel, outs, *args, scratch=(), flops=0):
    size = lambda xs: sum(x.size * x.dtype.itemsize for x in xs)
    return pl.pallas_call(
        kernel,
        out_shape=outs,
        in_specs=[VMEM] * len(args),
        out_specs=[VMEM] * len(outs),
        scratch_shapes=list(scratch),
        compiler_params=pltpu.CompilerParams(vmem_limit_bytes=24 * 1024 * 1024),
        cost_estimate=pl.CostEstimate(
            flops=flops, bytes_accessed=size(args) + size(outs), transcendentals=0
        ),
    )(*args)


def valid_kernel(p, valid_ref):
    for high, valid in enumerate(p.valid()):
        valid_ref[high] = jnp.where(valid, jnp.ones((8, 128), F32), 0.0)


def edge_of(p, valid_ref, slot, high, low):
    if p.n_edges == 2:
        return high if slot == 0 else low
    return jnp.where(valid_ref[0, 0:1, 0:1] == 0.0, high, low)


def pack_kernel(p, valid_ref, counts_ref, activity_ref, back_ref, edges_ref):
    lowest = valid_ref[0, 0:1, 0:1] == 0.0
    last = p.slices - 1
    activity = activity_ref[...].astype(F32)
    back = back_ref[...].astype(F32)
    for slot in range(p.n_edges):

        def edge(high, low):
            if p.n_edges == 2:
                return high if slot == 0 else low
            return jnp.where(lowest, high, low)

        for j in range(2):
            edges_ref[slot, j * p.each : (j + 1) * p.each] = edge(
                activity[:, last - 1 + j, :], activity[:, j, :]
            )
        for v in range(p.views):
            for r in range(p.n_view):
                at = p.edge_counts + (v * p.n_view + r) * p.each
                edges_ref[slot, at : at + p.each] = edge(
                    counts_ref[v, r, :, last, :], counts_ref[v, r, :, 0, :]
                ).astype(F32)
            edges_ref[slot, p.edge_back + v : p.edge_back + v + 1] = edge(
                back[v, last : last + 1], back[v, 0:1]
            )
        tail = p.edge_rows - p.edge_back - p.views
        if tail:
            edges_ref[slot, p.edge_back + p.views :] = jnp.zeros((tail, p.width), F32)


def payload_kernel(p, edges_ref, activity_ref, payload_ref):
    payload_ref[: p.block] = activity_ref[...].reshape(p.block, p.width)
    for e in range(p.n_edges):
        low = p.block + e * 2 * p.each
        payload_ref[low : low + 2 * p.each] = edges_ref[e, : 2 * p.each].astype(BF16)


def send_kernel(p, valid_ref, counts_ref, back_ref, values_ref, starts_ref, early_ref, *outs):
    at = lax.axis_index("view")
    row = lambda k: p.peer(at // p.pairs, k) * p.pairs + p.pairs - 1 - at % p.pairs
    last = p.slices - 1
    back = back_ref[...].astype(F32)
    for slot in range(p.n_edges):
        edge = functools.partial(edge_of, p, valid_ref, slot)
        pieces = []
        for v in range(p.views):
            for k in p.order:
                high, low = counts_ref[v, row(k), :, last, :], counts_ref[v, row(k), :, 0, :]
                pieces.append(edge(high, low).astype(F32))
        pieces += [edge(back[v, last : last + 1], back[v, 0:1]) for v in range(p.views)]
        tail = p.early_rows - p.early_back - p.views
        if tail:
            pieces.append(jnp.zeros((tail, p.width), F32))
        early_ref[slot] = jnp.concatenate(pieces, axis=0).astype(BF16)
    out = outs[0]
    out[: p.bands] = values_ref[...].reshape(p.bands, p.width)
    out[p.bands : p.starts] = back_ref[...].reshape(p.views * p.slices, p.width)
    starts = jnp.concatenate([starts_ref[t] for t in range(p.taps)], axis=0)
    pieces = [lax.shift_right_logical(starts, 7), starts & 127]
    tail = p.param_rows - p.starts - 2 * p.views * p.taps
    if tail:
        pieces.append(jnp.zeros((tail, p.width), I32))
    out[p.starts : p.param_rows] = jnp.concatenate(pieces, axis=0).astype(F32).astype(BF16)
    put_counts(p, 0, counts_ref, out)


def put_counts(p, m, counts_ref, out):
    at = lax.axis_index("view")
    ks = p.message_peers(m)
    for v in range(p.views):
        for i, k in enumerate(ks):
            row = p.peer(at // p.pairs, k) * p.pairs + p.pairs - 1 - at % p.pairs
            low = p.base(m) + (v * len(ks) + i) * p.block
            counts = counts_ref[v, row].astype(F32).astype(BF16)
            out[low : low + p.block] = counts.reshape(p.block, p.width)


def later_kernel(p, early_ref, counts_ref, wide_ref, *outs):
    wide_ref[...] = early_ref[...].astype(F32)
    for i, out in enumerate(outs):
        put_counts(p, 1 + i, counts_ref, out)


def place_bands(values, start):
    width = values.shape[1]
    moved = jnp.concatenate([values, jnp.zeros((8, width), F32)], axis=0)
    for step in (1, 2, 4):
        moved = jnp.where((start & step) != 0, pltpu.roll(moved, step, 0), moved)
    step = 8
    while step < width:
        longer = min(moved.shape[0] + step, width)
        zeros = jnp.zeros((step, width), F32)
        down = jnp.concatenate([zeros, moved], axis=0)[:longer]
        stay = jnp.concatenate([moved, zeros], axis=0)[:longer]
        moved = jnp.where((start & step) != 0, down, stay)
        step *= 2
    return moved.astype(BF16)


def matrix_kernel(p, params_ref, *refs):
    matrix_ref = refs[-1]
    starts = params_ref[p.starts : p.param_rows].astype(F32).astype(I32)
    n = p.views * p.taps
    starts = starts[:n] * 128 + starts[n : 2 * n]
    for v in range(p.views):
        for t in range(p.taps):
            at = v * p.taps + t
            values = params_ref[at * p.band : (at + 1) * p.band].astype(F32)
            at = t * p.views + v
            matrix_ref[v, t] = place_bands(values, starts[at : at + 1])


def place_source(p, blocks, lifted_ref, source_ref):
    rows = len(blocks) * p.each
    for i, block_ref in enumerate(blocks):
        low = i * p.each
        lifted_ref[low : low + p.each, 8 : 8 + p.slices, :] = (
            block_ref[: p.block].astype(F32).reshape(p.each, p.slices, p.width)
        )
        edges = block_ref[p.block :].astype(F32)
        for high, valid in enumerate(p.valid()):
            for j in range(2):
                at = (2 * min(high, p.n_edges - 1) + j) * p.each
                lifted_ref[low : low + p.each, (8 + p.slices if high else 6) + j, :] = jnp.where(
                    valid, edges[at : at + p.each], 0.0
                )
    main = rows * p.slices
    for t in range(p.taps):
        source_ref[t, :main] = (
            lifted_ref[:, 7 + t : 7 + t + p.slices, :].astype(BF16).reshape(main, p.width)
        )
        source_ref[t, main:] = jnp.concatenate(
            [lifted_ref[:, 6 + t, :], lifted_ref[:, 7 + p.slices + t, :]], axis=0
        ).astype(BF16)


class Rows:
    def __init__(self, p, stage, source_ref, ratio_ref, up_ref, down_ref):
        self.p, self.source_ref, self.ratio_ref, self.views = p, source_ref, ratio_ref, []
        self.up_ref, self.down_ref = up_ref, down_ref
        self.rows = len(p.stages[stage]) * p.each
        self.main, self.full = self.rows * p.slices, self.rows * (p.slices + 2)

    def view(self, matrix_ref, v, counts, back, edges, edge_backs):
        p, rows, main = self.p, self.rows, self.main
        expected = None
        for t in range(p.taps):
            term = jnp.dot(self.source_ref[t], matrix_ref[v, t], preferred_element_type=F32)
            expected = term if expected is None else expected + term
        inner = expected[:main].reshape(rows, p.slices, p.width) + back[None]
        ratio = counts.astype(F32).reshape(rows, p.slices, p.width) / inner - 1.0
        n = len(self.views)
        self.ratio_ref[n, :main] = ratio.astype(BF16).reshape(main, p.width)
        outer = []
        for high, valid in enumerate(p.valid()):
            low = main + high * rows
            e = min(high, p.n_edges - 1)
            ratio = edges[e] / (expected[low : low + rows] + edge_backs[e]) - 1.0
            outer.append(jnp.where(valid, ratio, 0.0))
        self.ratio_ref[n, main:] = jnp.concatenate(outer, axis=0).astype(BF16)
        self.views.append((matrix_ref, v))

    def project(self, tap, stop):
        total = None
        for n, (matrix_ref, v) in enumerate(self.views):
            term = lax.dot_general(
                self.ratio_ref[n, :stop],
                matrix_ref[v, tap],
                (((1,), (1,)), ((), ())),
                preferred_element_type=F32,
            )
            total = term if total is None else total + term
        return total

    def gradient(self):
        p, rows, main, full = self.p, self.rows, self.main, self.full
        shape = (rows, p.slices, p.width)
        part = self.project(0, full)
        self.up_ref[:, : p.slices, :] = part[:main].reshape(shape)
        self.up_ref[:, p.slices, :] = part[main + rows :]
        part = self.project(2, full)
        self.down_ref[:, 8 : 8 + p.slices, :] = part[:main].reshape(shape)
        self.down_ref[:, 7, :] = part[main : main + rows]
        total = self.project(1, main).reshape(shape)
        return total + self.up_ref[:, 1 : 1 + p.slices, :] + self.down_ref[:, 7 : 7 + p.slices, :]


def own_kernel(p, stage, counts_ref, edges_ref, back_ref, matrix_ref, *refs):
    ks = p.stages[stage]
    blocks, refs = refs[: len(ks)], refs[len(ks) :]
    refs = refs[min(stage, 1) :]
    source_ref, total_ref, lifted_ref, *scratch = refs
    place_source(p, blocks, lifted_ref, source_ref)
    work = Rows(p, stage, source_ref, *scratch)
    at = lax.axis_index("view")
    places = [p.peer(at // p.pairs, k) * p.pairs + at % p.pairs for k in ks]
    for v in range(p.views):
        edges, edge_backs = [], []
        for e in range(p.n_edges):
            pieces = []
            for row in places:
                start = p.edge_counts + (v * p.n_view + row) * p.each
                pieces.append(edges_ref[e, pl.ds(pl.multiple_of(start, p.each), p.each), :])
            edges.append(jnp.concatenate(pieces, axis=0))
            edge_backs.append(edges_ref[e, p.edge_back + v : p.edge_back + v + 1])
        counts = jnp.concatenate([counts_ref[v, row] for row in places], axis=0)
        work.view(matrix_ref, v, counts, back_ref[v].astype(F32), edges, edge_backs)
    total_ref[...] = work.gradient()


def their_kernel(p, stage, after, source_ref, total_ref, *refs):
    ks = p.stages[stage]
    refs = refs[after:]
    total = total_ref[...]
    if p.pairs == 2:
        (message_ref, first_ref, early_ref, matrix_ref), refs = refs[:4], refs[4:]
    outs, scratch = refs[: len(ks)], refs[len(ks) :]
    if p.pairs == 2:
        work = Rows(p, stage, source_ref, *scratch)
        (m,) = [m for m, stages in enumerate(p.messages) if stage in stages]
        peers = p.message_peers(m)
        skip = peers.index(ks[0])
        came = [early_ref[e].astype(F32) for e in range(p.n_edges)]
        for v in range(p.views):
            low = (v * p.line + p.order.index(ks[0])) * p.each
            edges = [x[low : low + work.rows] for x in came]
            edge_backs = [x[p.early_back + v : p.early_back + v + 1] for x in came]
            low = p.base(m) + (v * len(peers) + skip) * p.block
            back = first_ref[p.bands + v * p.slices : p.bands + (v + 1) * p.slices].astype(F32)
            counts = message_ref[low : low + work.main]
            work.view(matrix_ref, v, counts, back, edges, edge_backs)
        total = total + work.gradient()
    for i, out in enumerate(outs):
        part = total[i * p.each : (i + 1) * p.each]
        if ks[i] == 0:
            out[...] = part
        else:
            encode(p, part, out)


def encode(p, x, out_ref):
    most = jnp.maximum(jnp.max(jnp.abs(x), axis=1), 1e-30)
    power = jnp.ceil(jnp.log2(most) * STEPS)
    codes = jnp.round(x * (FULL * jnp.exp2(power * (-1.0 / STEPS)))[:, None, :])
    out_ref[: p.block] = codes.reshape(p.block, p.width).astype(I32).astype(I16)
    tail = padded_16(p.each) - p.each
    if tail:
        power = jnp.concatenate([power, jnp.zeros((tail, p.width), F32)], axis=0)
    out_ref[p.block :] = power.astype(I32).astype(I16)


def decode(p, in_ref):
    power = in_ref[p.block :].astype(I32).astype(F32)[: p.each]
    scale = jnp.exp2(power * (1.0 / STEPS)) * (1.0 / FULL)
    codes = in_ref[: p.block].astype(I32).astype(F32)
    return codes.reshape(p.each, p.slices, p.width) * scale[:, None, :]


def sum_kernel(p, coded, *refs):
    total = None
    for i, ref in enumerate(refs[:-1]):
        term = decode(p, ref) if i < coded else ref[...]
        total = term if total is None else total + term
    refs[-1][...] = total


def per_device(activity, histo_counts, background, blur_values, band_start):
    p = Plan(activity, histo_counts, blur_values)
    shape = jax.ShapeDtypeStruct
    part = lambda kernel, *static: functools.partial(kernel, p, *static)
    width = p.width
    other = [(i, i ^ 1) for i in range(p.n_view)]

    counts = histo_counts.reshape(p.views, p.n_view, p.each, p.slices, width)
    values = jnp.swapaxes(blur_values, 2, 3)
    starts = jnp.swapaxes(band_start, 0, 1)
    (valid,) = call(part(valid_kernel), [shape((2, 8, 128), F32)], flops=2 * 10**9)
    (edges,) = call(
        part(pack_kernel),
        [shape((p.n_edges, p.edge_rows, width), F32)],
        valid, counts, activity, background,
    )
    def swapped(x, flip):
        n = p.n_slab
        pairs = [(i, i ^ flip) for i in range(p.n_view)]
        up = [(i * n + s, j * n + s + 1) for i, j in pairs for s in range(n - 1)]
        down = [(i * n + s + 1, j * n + s) for i, j in pairs for s in range(n - 1)]
        send = lambda part, moves: lax.ppermute(part, ("view", "slab"), moves)
        if n > 2:
            return jnp.stack([send(x[0], up), send(x[1], down)])
        return send(x, up + down) if n == 2 else x

    outs = [shape((p.n_edges, p.early_rows, width), BF16)]
    outs += [shape((p.message_rows(0), width), BF16)]
    early, *sent = call(part(send_kernel), outs, valid, counts, background, values, starts)
    if p.pairs == 2:
        early = swapped(early, 1)
        theirs = [lax.ppermute(x, "view", other) for x in sent]
        outs = [shape(early.shape, F32)]
        outs += [shape((p.message_rows(m), width), BF16) for m in range(1, len(p.messages))]
        early, *later = call(part(later_kernel), outs, early, counts, flops=LONG)
        theirs += [lax.ppermute(x, "view", other) for x in later]
    edges = swapped(edges, 0)
    (payload,) = call(
        part(payload_kernel),
        [shape((p.block + 2 * p.n_edges * p.each, width), BF16)],
        edges, activity,
    )
    blocks = {0: payload}
    for k in [k for ks in p.stages for k in ks if k]:
        blocks[k] = lax.ppermute(payload, "view", p.across(k, False))

    matrices = shape((p.views, p.taps, width, width), BF16)
    (matrix,) = call(part(matrix_kernel), [matrices], sent[0])
    if p.pairs == 2:
        (their_matrix,) = call(part(matrix_kernel), [matrices], theirs[0])

    code = shape((p.block + padded_16(p.each), width), I16)
    plain = shape((p.each, p.slices, width), F32)
    terms, firsts = {}, []
    for stage, ks in enumerate(p.stages):
        rows = len(ks) * p.each
        full = rows * (p.slices + 2)
        before = list(terms.values())[-1:] if stage > 1 else firsts[:1]
        scratch = [
            pltpu.VMEM((p.views, full, width), BF16),
            pltpu.VMEM((rows, p.slices + 8, width), F32),
            pltpu.VMEM((rows, p.slices + 8, width), F32),
        ]
        own = call(
            part(own_kernel, stage),
            [shape((p.taps, full, width), BF16), shape((rows, p.slices, width), F32)],
            counts, edges, background, matrix, *[blocks[k] for k in ks], *before,
            scratch=[pltpu.VMEM((rows, p.slices + 16, width), F32)] + scratch,
            flops=LONG if stage == 0 else 4 * p.views * p.taps * full * width * width,
        )
        firsts.append(own[1])
        before = list(terms.values())[-1:]
        args = [*own, *before]
        if p.pairs == 2:
            (m,) = [m for m, stages in enumerate(p.messages) if stage in stages]
            args += [theirs[m], theirs[0], early, their_matrix]
        outs = call(
            part(their_kernel, stage, len(before)),
            [code if k else plain for k in ks],
            *args,
            scratch=[
                pltpu.VMEM((p.views, full, width), BF16),
                pltpu.VMEM((rows, p.slices + 8, width), F32),
                pltpu.VMEM((rows, p.slices + 8, width), F32),
            ],
            flops=4 * p.views * p.taps * full * width * width,
        )
        terms.update(zip(ks, outs))
    total = []
    for m in range(len(p.messages)):
        came = [
            lax.ppermute(terms[k], "view", p.across(k, True)) for k in p.message_peers(m) if k
        ]
        if m == len(p.messages) - 1:
            total = total + [terms[0]]
        total = list(call(part(sum_kernel, len(came)), [plain], *came, *total))
    return total[0]


def solution(mesh):
    placed = (
        P(("parts", "view"), "slab", None),
        P(("parts", "view"), None, "slab", None),
        P(("parts", "view"), "slab", None),
        P("view", None, None, None),
        P("view", None, None),
    )
    return jax.shard_map(
        per_device,
        mesh=mesh,
        in_specs=placed,
        out_specs=P(("parts", "view"), "slab", None),
        check_vma=False,
    )
```

```python
import functools

import jax
import jax.numpy as jnp
from jax import lax
from jax.experimental import pallas as pl
from jax.experimental.pallas import tpu as pltpu
from jax.sharding import PartitionSpec as P

VMEM = pl.BlockSpec(memory_space=pltpu.VMEM)
BF16, F32, I16, I32 = jnp.bfloat16, jnp.float32, jnp.int16, jnp.int32
LONG = 8 * 10**9
FULL, STEPS = 32700.0, 64.0


def padded_16(rows):
    return -(-rows // 16) * 16


class Plan:
    def __init__(self, activity, histo_counts, blur_values):
        self.each, self.slices, self.width = activity.shape
        self.views, self.taps, _, self.band = blur_values.shape
        self.n_slab = lax.axis_size("slab")
        self.n_view = lax.axis_size("view")
        self.pairs = 2 if self.n_view % 2 == 0 else 1
        self.line = self.n_view // self.pairs
        self.block = self.each * self.slices
        self.n_edges = 2 if self.n_slab > 2 else 1
        half = self.line // 2
        stages = [s for s in (range(half, self.line), range(1, half), range(1)) if len(s)]
        self.stages = [list(s) for s in stages] if half else [[0]]
        self.messages = [[0], list(range(1, len(self.stages)))][: len(self.stages)]
        self.edge_counts = 2 * self.each
        self.edge_back = self.edge_counts + self.views * self.n_view * self.each
        self.edge_rows = self.edge_back + padded_16(self.views)
        self.all_bands = self.views * self.taps * self.band
        self.start_rows = padded_16(2 * self.views * self.taps)
        self.split = self.n_slab == 2 and self.all_bands % 32 == 0
        self.bands = 0 if self.split else self.all_bands
        self.starts = self.bands + self.views * self.slices
        self.param_rows = self.starts + (0 if self.split else self.start_rows)
        self.order = [k for s in self.stages for k in s]
        self.early_back = self.views * self.line * self.each
        self.early_starts = padded_16(self.early_back + self.views)
        self.early_bands = self.early_starts + self.start_rows
        self.half = self.all_bands // 2
        self.early_rows = self.early_bands + self.half if self.split else self.early_starts

    def message_peers(self, m):
        return [k for s in self.messages[m] for k in self.stages[s]]

    def base(self, m):
        return 0 if m else self.param_rows

    def message_rows(self, m):
        return self.base(m) + self.views * len(self.message_peers(m)) * self.block

    def peer(self, at, k):
        xor = self.line & (self.line - 1) == 0
        return at ^ k if xor else (at + k) % self.line

    def across(self, k, towards):
        g = self.pairs
        moves = [(i, self.peer(i // g, k) * g + i % g) for i in range(self.n_view)]
        return moves if towards else [(j, i) for i, j in moves]

    def valid(self):
        slab = lax.axis_index("slab")
        return (slab > 0, slab < self.n_slab - 1)


def call(kernel, outs, *args, scratch=(), flops=0):
    size = lambda xs: sum(x.size * x.dtype.itemsize for x in xs)
    return pl.pallas_call(
        kernel,
        out_shape=outs,
        in_specs=[VMEM] * len(args),
        out_specs=[VMEM] * len(outs),
        scratch_shapes=list(scratch),
        compiler_params=pltpu.CompilerParams(vmem_limit_bytes=24 * 1024 * 1024),
        cost_estimate=pl.CostEstimate(
            flops=flops, bytes_accessed=size(args) + size(outs), transcendentals=0
        ),
    )(*args)


def valid_kernel(p, valid_ref):
    for high, valid in enumerate(p.valid()):
        valid_ref[high] = jnp.where(valid, jnp.ones((8, 128), F32), 0.0)


def edge_of(p, valid_ref, slot, high, low):
    if p.n_edges == 2:
        return high if slot == 0 else low
    return jnp.where(valid_ref[0, 0:1, 0:1] == 0.0, high, low)


def pack_kernel(p, valid_ref, counts_ref, activity_ref, back_ref, edges_ref):
    lowest = valid_ref[0, 0:1, 0:1] == 0.0
    last = p.slices - 1
    activity = activity_ref[...].astype(F32)
    back = back_ref[...].astype(F32)
    for slot in range(p.n_edges):

        def edge(high, low):
            if p.n_edges == 2:
                return high if slot == 0 else low
            return jnp.where(lowest, high, low)

        for j in range(2):
            edges_ref[slot, j * p.each : (j + 1) * p.each] = edge(
                activity[:, last - 1 + j, :], activity[:, j, :]
            )
        for v in range(p.views):
            for r in range(p.n_view):
                at = p.edge_counts + (v * p.n_view + r) * p.each
                edges_ref[slot, at : at + p.each] = edge(
                    counts_ref[v, r, :, last, :], counts_ref[v, r, :, 0, :]
                ).astype(F32)
            edges_ref[slot, p.edge_back + v : p.edge_back + v + 1] = edge(
                back[v, last : last + 1], back[v, 0:1]
            )
        tail = p.edge_rows - p.edge_back - p.views
        if tail:
            edges_ref[slot, p.edge_back + p.views :] = jnp.zeros((tail, p.width), F32)


def payload_kernel(p, edges_ref, activity_ref, payload_ref):
    payload_ref[: p.block] = activity_ref[...].reshape(p.block, p.width)
    for e in range(p.n_edges):
        low = p.block + e * 2 * p.each
        payload_ref[low : low + 2 * p.each] = edges_ref[e, : 2 * p.each].astype(BF16)


def send_kernel(p, valid_ref, counts_ref, back_ref, values_ref, starts_ref, early_ref, *outs):
    at = lax.axis_index("view")
    row = lambda k: p.peer(at // p.pairs, k) * p.pairs + p.pairs - 1 - at % p.pairs
    last = p.slices - 1
    back = back_ref[...].astype(F32)
    for slot in range(p.n_edges):
        edge = functools.partial(edge_of, p, valid_ref, slot)
        pieces = []
        for v in range(p.views):
            for k in p.order:
                high, low = counts_ref[v, row(k), :, last, :], counts_ref[v, row(k), :, 0, :]
                pieces.append(edge(high, low).astype(F32))
        pieces += [edge(back[v, last : last + 1], back[v, 0:1]) for v in range(p.views)]
        tail = p.early_starts - p.early_back - p.views
        if tail:
            pieces.append(jnp.zeros((tail, p.width), F32))
        early_ref[slot, : p.early_starts] = jnp.concatenate(pieces, axis=0).astype(BF16)
    out = outs[0]
    values = values_ref[...].reshape(p.all_bands, p.width)
    out[p.bands : p.starts] = back_ref[...].reshape(p.views * p.slices, p.width)
    starts = jnp.concatenate([starts_ref[t] for t in range(p.taps)], axis=0)
    pieces = [lax.shift_right_logical(starts, 7), starts & 127]
    tail = p.start_rows - 2 * p.views * p.taps
    if tail:
        pieces.append(jnp.zeros((tail, p.width), I32))
    starts = jnp.concatenate(pieces, axis=0).astype(F32).astype(BF16)
    if p.split:
        lowest = valid_ref[0, 0:1, 0:1] == 0.0
        values = values.astype(F32)
        early_ref[0, p.early_starts : p.early_bands] = starts
        early_ref[0, p.early_bands :] = jnp.where(lowest, values[: p.half], values[p.half :]).astype(BF16)
    else:
        out[: p.bands] = values
        out[p.starts : p.param_rows] = starts
    put_counts(p, 0, counts_ref, out)


def put_counts(p, m, counts_ref, out):
    at = lax.axis_index("view")
    ks = p.message_peers(m)
    for v in range(p.views):
        for i, k in enumerate(ks):
            row = p.peer(at // p.pairs, k) * p.pairs + p.pairs - 1 - at % p.pairs
            low = p.base(m) + (v * len(ks) + i) * p.block
            counts = counts_ref[v, row].astype(F32).astype(BF16)
            out[low : low + p.block] = counts.reshape(p.block, p.width)


def later_kernel(p, early_ref, counts_ref, block_ref, wide_ref, half_ref, *outs):
    wide_ref[...] = early_ref[...].astype(F32)
    if p.split:
        half_ref[...] = early_ref[0, p.early_bands :]
    for i, out in enumerate(outs):
        put_counts(p, 1 + i, counts_ref, out)


def place_bands(values, start):
    width = values.shape[1]
    moved = jnp.concatenate([values, jnp.zeros((8, width), F32)], axis=0)
    for step in (1, 2, 4):
        moved = jnp.where((start & step) != 0, pltpu.roll(moved, step, 0), moved)
    step = 8
    while step < width:
        longer = min(moved.shape[0] + step, width)
        zeros = jnp.zeros((step, width), F32)
        down = jnp.concatenate([zeros, moved], axis=0)[:longer]
        stay = jnp.concatenate([moved, zeros], axis=0)[:longer]
        moved = jnp.where((start & step) != 0, down, stay)
        step *= 2
    return moved.astype(BF16)


def own_matrix_kernel(p, values_ref, starts_ref, matrix_ref):
    for v in range(p.views):
        for t in range(p.taps):
            matrix_ref[v, t] = place_bands(values_ref[v, t].astype(F32), starts_ref[t, v : v + 1])


def their_matrix_kernel(p, valid_ref, params_ref, *refs):
    matrix_ref = refs[-1]
    if p.split:
        lowest = valid_ref[0, 0:1, 0:1] == 0.0
        here, rest = params_ref[0, p.early_bands :], refs[0][...].astype(F32)
        values = [jnp.where(lowest, rest, here), jnp.where(lowest, here, rest)]
        values = jnp.concatenate(values, axis=0)
        starts = params_ref[0, p.early_starts : p.early_bands].astype(I32)
    else:
        values = params_ref[: p.bands].astype(F32)
        starts = params_ref[p.starts : p.param_rows].astype(F32).astype(I32)
    n = p.views * p.taps
    starts = starts[:n] * 128 + starts[n : 2 * n]
    for v in range(p.views):
        for t in range(p.taps):
            low, at = (v * p.taps + t) * p.band, t * p.views + v
            matrix_ref[v, t] = place_bands(values[low : low + p.band], starts[at : at + 1])


def place_source(p, blocks, lifted_ref, source_ref):
    rows = len(blocks) * p.each
    for i, block_ref in enumerate(blocks):
        low = i * p.each
        lifted_ref[low : low + p.each, 8 : 8 + p.slices, :] = (
            block_ref[: p.block].astype(F32).reshape(p.each, p.slices, p.width)
        )
        edges = block_ref[p.block :].astype(F32)
        for high, valid in enumerate(p.valid()):
            for j in range(2):
                at = (2 * min(high, p.n_edges - 1) + j) * p.each
                lifted_ref[low : low + p.each, (8 + p.slices if high else 6) + j, :] = jnp.where(
                    valid, edges[at : at + p.each], 0.0
                )
    main = rows * p.slices
    for t in range(p.taps):
        source_ref[t, :main] = (
            lifted_ref[:, 7 + t : 7 + t + p.slices, :].astype(BF16).reshape(main, p.width)
        )
        source_ref[t, main:] = jnp.concatenate(
            [lifted_ref[:, 6 + t, :], lifted_ref[:, 7 + p.slices + t, :]], axis=0
        ).astype(BF16)


class Rows:
    def __init__(self, p, stage, source_ref, ratio_ref, up_ref, down_ref):
        self.p, self.source_ref, self.ratio_ref, self.views = p, source_ref, ratio_ref, []
        self.up_ref, self.down_ref = up_ref, down_ref
        self.rows = len(p.stages[stage]) * p.each
        self.main, self.full = self.rows * p.slices, self.rows * (p.slices + 2)

    def view(self, matrix_ref, v, counts, back, edges, edge_backs):
        p, rows, main = self.p, self.rows, self.main
        expected = None
        for t in range(p.taps):
            term = jnp.dot(self.source_ref[t], matrix_ref[v, t], preferred_element_type=F32)
            expected = term if expected is None else expected + term
        inner = expected[:main].reshape(rows, p.slices, p.width) + back[None]
        ratio = counts.astype(F32).reshape(rows, p.slices, p.width) / inner - 1.0
        n = len(self.views)
        self.ratio_ref[n, :main] = ratio.astype(BF16).reshape(main, p.width)
        outer = []
        for high, valid in enumerate(p.valid()):
            low = main + high * rows
            e = min(high, p.n_edges - 1)
            ratio = edges[e] / (expected[low : low + rows] + edge_backs[e]) - 1.0
            outer.append(jnp.where(valid, ratio, 0.0))
        self.ratio_ref[n, main:] = jnp.concatenate(outer, axis=0).astype(BF16)
        self.views.append((matrix_ref, v))

    def project(self, tap, stop):
        total = None
        for n, (matrix_ref, v) in enumerate(self.views):
            term = lax.dot_general(
                self.ratio_ref[n, :stop],
                matrix_ref[v, tap],
                (((1,), (1,)), ((), ())),
                preferred_element_type=F32,
            )
            total = term if total is None else total + term
        return total

    def gradient(self):
        p, rows, main, full = self.p, self.rows, self.main, self.full
        shape = (rows, p.slices, p.width)
        part = self.project(0, full)
        self.up_ref[:, : p.slices, :] = part[:main].reshape(shape)
        self.up_ref[:, p.slices, :] = part[main + rows :]
        part = self.project(2, full)
        self.down_ref[:, 8 : 8 + p.slices, :] = part[:main].reshape(shape)
        self.down_ref[:, 7, :] = part[main : main + rows]
        total = self.project(1, main).reshape(shape)
        return total + self.up_ref[:, 1 : 1 + p.slices, :] + self.down_ref[:, 7 : 7 + p.slices, :]


def own_kernel(p, stage, counts_ref, edges_ref, back_ref, matrix_ref, *refs):
    ks = p.stages[stage]
    blocks, refs = refs[: len(ks)], refs[len(ks) :]
    refs = refs[min(stage, 1) :]
    source_ref, total_ref, lifted_ref, *scratch = refs
    place_source(p, blocks, lifted_ref, source_ref)
    work = Rows(p, stage, source_ref, *scratch)
    at = lax.axis_index("view")
    places = [p.peer(at // p.pairs, k) * p.pairs + at % p.pairs for k in ks]
    for v in range(p.views):
        edges, edge_backs = [], []
        for e in range(p.n_edges):
            pieces = []
            for row in places:
                start = p.edge_counts + (v * p.n_view + row) * p.each
                pieces.append(edges_ref[e, pl.ds(pl.multiple_of(start, p.each), p.each), :])
            edges.append(jnp.concatenate(pieces, axis=0))
            edge_backs.append(edges_ref[e, p.edge_back + v : p.edge_back + v + 1])
        counts = jnp.concatenate([counts_ref[v, row] for row in places], axis=0)
        work.view(matrix_ref, v, counts, back_ref[v].astype(F32), edges, edge_backs)
    total_ref[...] = work.gradient()


def their_kernel(p, stage, after, source_ref, total_ref, *refs):
    ks = p.stages[stage]
    refs = refs[after:]
    total = total_ref[...]
    if p.pairs == 2:
        (message_ref, first_ref, early_ref, matrix_ref), refs = refs[:4], refs[4:]
    outs, scratch = refs[: len(ks)], refs[len(ks) :]
    if p.pairs == 2:
        work = Rows(p, stage, source_ref, *scratch)
        (m,) = [m for m, stages in enumerate(p.messages) if stage in stages]
        peers = p.message_peers(m)
        skip = peers.index(ks[0])
        came = [early_ref[e].astype(F32) for e in range(p.n_edges)]
        for v in range(p.views):
            low = (v * p.line + p.order.index(ks[0])) * p.each
            edges = [x[low : low + work.rows] for x in came]
            edge_backs = [x[p.early_back + v : p.early_back + v + 1] for x in came]
            low = p.base(m) + (v * len(peers) + skip) * p.block
            back = first_ref[p.bands + v * p.slices : p.bands + (v + 1) * p.slices].astype(F32)
            counts = message_ref[low : low + work.main]
            work.view(matrix_ref, v, counts, back, edges, edge_backs)
        total = total + work.gradient()
    for i, out in enumerate(outs):
        part = total[i * p.each : (i + 1) * p.each]
        if ks[i] == 0:
            out[...] = part
        else:
            encode(p, part, out)


def encode(p, x, out_ref):
    most = jnp.maximum(jnp.max(jnp.abs(x), axis=1), 1e-30)
    power = jnp.ceil(jnp.log2(most) * STEPS)
    codes = jnp.round(x * (FULL * jnp.exp2(power * (-1.0 / STEPS)))[:, None, :])
    out_ref[: p.block] = codes.reshape(p.block, p.width).astype(I32).astype(I16)
    tail = padded_16(p.each) - p.each
    if tail:
        power = jnp.concatenate([power, jnp.zeros((tail, p.width), F32)], axis=0)
    out_ref[p.block :] = power.astype(I32).astype(I16)


def decode(p, in_ref):
    power = in_ref[p.block :].astype(I32).astype(F32)[: p.each]
    scale = jnp.exp2(power * (1.0 / STEPS)) * (1.0 / FULL)
    codes = in_ref[: p.block].astype(I32).astype(F32)
    return codes.reshape(p.each, p.slices, p.width) * scale[:, None, :]


def sum_kernel(p, coded, *refs):
    total = None
    for i, ref in enumerate(refs[:-1]):
        term = decode(p, ref) if i < coded else ref[...]
        total = term if total is None else total + term
    refs[-1][...] = total


def per_device(activity, histo_counts, background, blur_values, band_start):
    p = Plan(activity, histo_counts, blur_values)
    shape = jax.ShapeDtypeStruct
    part = lambda kernel, *static: functools.partial(kernel, p, *static)
    width = p.width
    other = [(i, i ^ 1) for i in range(p.n_view)]

    counts = histo_counts.reshape(p.views, p.n_view, p.each, p.slices, width)
    values = jnp.swapaxes(blur_values, 2, 3)
    starts = jnp.swapaxes(band_start, 0, 1)
    (valid,) = call(part(valid_kernel), [shape((2, 8, 128), F32)], flops=2 * 10**9)
    (edges,) = call(
        part(pack_kernel),
        [shape((p.n_edges, p.edge_rows, width), F32)],
        valid, counts, activity, background,
    )
    def swapped(x, flip):
        n = p.n_slab
        pairs = [(i, i ^ flip) for i in range(p.n_view)]
        up = [(i * n + s, j * n + s + 1) for i, j in pairs for s in range(n - 1)]
        down = [(i * n + s + 1, j * n + s) for i, j in pairs for s in range(n - 1)]
        send = lambda part, moves: lax.ppermute(part, ("view", "slab"), moves)
        if n > 2:
            return jnp.stack([send(x[0], up), send(x[1], down)])
        return send(x, up + down) if n == 2 else x

    outs = [shape((p.n_edges, p.early_rows, width), BF16)]
    outs += [shape((p.message_rows(0), width), BF16)]
    early, *sent = call(part(send_kernel), outs, valid, counts, background, values, starts)
    if p.pairs == 2:
        early = swapped(early, 1)
        theirs = [lax.ppermute(x, "view", other) for x in sent]
    edges = swapped(edges, 0)
    (payload,) = call(
        part(payload_kernel),
        [shape((p.block + 2 * p.n_edges * p.each, width), BF16)],
        edges, activity,
    )
    blocks = {0: payload}
    for k in [k for ks in p.stages for k in ks if k]:
        blocks[k] = lax.ppermute(payload, "view", p.across(k, False))

    if p.pairs == 2:
        outs = [shape(early.shape, F32), shape((p.half, width), BF16)]
        outs += [shape((p.message_rows(m), width), BF16) for m in range(1, len(p.messages))]
        early, rest, *later = call(part(later_kernel), outs, early, counts, blocks[p.stages[0][0]], flops=LONG)
        theirs += [lax.ppermute(x, "view", other) for x in later]
        if p.split:
            rest = swapped(rest, 0)
    matrices = shape((p.views, p.taps, width, width), BF16)
    (matrix,) = call(part(own_matrix_kernel), [matrices], values, starts)
    if p.pairs == 2:
        made_of = [early, rest] if p.split else theirs[:1]
        (their_matrix,) = call(part(their_matrix_kernel), [matrices], valid, *made_of, flops=0)

    code = shape((p.block + padded_16(p.each), width), I16)
    plain = shape((p.each, p.slices, width), F32)
    terms = {}
    for stage, ks in enumerate(p.stages):
        rows = len(ks) * p.each
        full = rows * (p.slices + 2)
        before = list(terms.values())[-1:]
        scratch = [
            pltpu.VMEM((p.views, full, width), BF16),
            pltpu.VMEM((rows, p.slices + 8, width), F32),
            pltpu.VMEM((rows, p.slices + 8, width), F32),
        ]
        own = call(
            part(own_kernel, stage),
            [shape((p.taps, full, width), BF16), shape((rows, p.slices, width), F32)],
            counts, edges, background, matrix, *[blocks[k] for k in ks], *before,
            scratch=[pltpu.VMEM((rows, p.slices + 16, width), F32)] + scratch,
            flops=LONG if stage == 0 else 4 * p.views * p.taps * full * width * width,
        )
        before = list(terms.values())[-1:]
        args = [*own, *before]
        if p.pairs == 2:
            (m,) = [m for m, stages in enumerate(p.messages) if stage in stages]
            args += [theirs[m], theirs[0], early, their_matrix]
        outs = call(
            part(their_kernel, stage, len(before)),
            [code if k else plain for k in ks],
            *args,
            scratch=[
                pltpu.VMEM((p.views, full, width), BF16),
                pltpu.VMEM((rows, p.slices + 8, width), F32),
                pltpu.VMEM((rows, p.slices + 8, width), F32),
            ],
            flops=4 * p.views * p.taps * full * width * width,
        )
        terms.update(zip(ks, outs))
    total = [terms[0]]
    for m in range(len(p.messages)):
        came = [
            lax.ppermute(terms[k], "view", p.across(k, True)) for k in p.message_peers(m) if k
        ]
        total = list(call(part(sum_kernel, len(came)), [plain], *came, *total))
    return total[0]


def solution(mesh):
    placed = (
        P(("parts", "view"), "slab", None),
        P(("parts", "view"), None, "slab", None),
        P(("parts", "view"), "slab", None),
        P("view", None, None, None),
        P("view", None, None),
    )
    return jax.shard_map(
        per_device,
        mesh=mesh,
        in_specs=placed,
        out_specs=P(("parts", "view"), "slab", None),
        check_vma=False,
    )
```

```python
import functools

import jax
import jax.numpy as jnp
from jax import lax
from jax.experimental import pallas as pl
from jax.experimental.pallas import tpu as pltpu
from jax.sharding import PartitionSpec as P

VMEM = pl.BlockSpec(memory_space=pltpu.VMEM)
BF16, F32, I16, I32 = jnp.bfloat16, jnp.float32, jnp.int16, jnp.int32
LONG = 8 * 10**9
FULL, STEPS = 32700.0, 64.0


def padded_16(rows):
    return -(-rows // 16) * 16


class Plan:
    def __init__(self, activity, histo_counts, blur_values):
        self.each, self.slices, self.width = activity.shape
        self.views, self.taps, _, self.band = blur_values.shape
        self.n_slab = lax.axis_size("slab")
        self.n_view = lax.axis_size("view")
        self.pairs = 2 if self.n_view % 2 == 0 else 1
        self.line = self.n_view // self.pairs
        self.block = self.each * self.slices
        self.n_edges = 2 if self.n_slab > 2 else 1
        half = self.line // 2
        stages = [s for s in (range(half, self.line), range(1, half), range(1)) if len(s)]
        self.stages = [list(s) for s in stages] if half else [[0]]
        self.messages = [[0], list(range(1, len(self.stages)))][: len(self.stages)]
        self.edge_counts = 2 * self.each
        self.edge_back = self.edge_counts + self.views * self.n_view * self.each
        self.edge_rows = self.edge_back + padded_16(self.views)
        self.all_bands = self.views * self.taps * self.band
        self.start_rows = padded_16(2 * self.views * self.taps)
        self.split = self.n_slab == 2 and self.all_bands % 32 == 0
        self.bands = 0 if self.split else self.all_bands
        self.starts = self.bands + self.views * self.slices
        self.param_rows = self.starts + (0 if self.split else self.start_rows)
        self.order = [k for s in self.stages for k in s]
        self.early_back = self.views * self.line * self.each
        self.early_starts = padded_16(self.early_back + self.views)
        self.early_bands = self.early_starts + self.start_rows
        self.half = self.all_bands // 2
        self.early_rows = self.early_bands + self.half if self.split else self.early_starts

    def message_peers(self, m):
        return [k for s in self.messages[m] for k in self.stages[s]]

    def base(self, m):
        return 0 if m else self.param_rows

    def message_rows(self, m):
        return self.base(m) + self.views * len(self.message_peers(m)) * self.block

    def peer(self, at, k):
        xor = self.line & (self.line - 1) == 0
        return at ^ k if xor else (at + k) % self.line

    def across(self, k, towards):
        g = self.pairs
        moves = [(i, self.peer(i // g, k) * g + i % g) for i in range(self.n_view)]
        return moves if towards else [(j, i) for i, j in moves]

    def valid(self):
        slab = lax.axis_index("slab")
        return (slab > 0, slab < self.n_slab - 1)


def call(kernel, outs, *args, scratch=(), flops=0):
    size = lambda xs: sum(x.size * x.dtype.itemsize for x in xs)
    return pl.pallas_call(
        kernel,
        out_shape=outs,
        in_specs=[VMEM] * len(args),
        out_specs=[VMEM] * len(outs),
        scratch_shapes=list(scratch),
        compiler_params=pltpu.CompilerParams(vmem_limit_bytes=24 * 1024 * 1024),
        cost_estimate=pl.CostEstimate(
            flops=flops, bytes_accessed=size(args) + size(outs), transcendentals=0
        ),
    )(*args)


def valid_kernel(p, valid_ref):
    for high, valid in enumerate(p.valid()):
        valid_ref[high] = jnp.where(valid, jnp.ones((8, 128), F32), 0.0)


def edge_of(p, valid_ref, slot, high, low):
    if p.n_edges == 2:
        return high if slot == 0 else low
    return jnp.where(valid_ref[0, 0:1, 0:1] == 0.0, high, low)


def pack_kernel(p, valid_ref, counts_ref, activity_ref, back_ref, edges_ref):
    lowest = valid_ref[0, 0:1, 0:1] == 0.0
    last = p.slices - 1
    activity = activity_ref[...].astype(F32)
    back = back_ref[...].astype(F32)
    for slot in range(p.n_edges):

        def edge(high, low):
            if p.n_edges == 2:
                return high if slot == 0 else low
            return jnp.where(lowest, high, low)

        for j in range(2):
            edges_ref[slot, j * p.each : (j + 1) * p.each] = edge(
                activity[:, last - 1 + j, :], activity[:, j, :]
            )
        for v in range(p.views):
            for r in range(p.n_view):
                at = p.edge_counts + (v * p.n_view + r) * p.each
                edges_ref[slot, at : at + p.each] = edge(
                    counts_ref[v, r, :, last, :], counts_ref[v, r, :, 0, :]
                ).astype(F32)
            edges_ref[slot, p.edge_back + v : p.edge_back + v + 1] = edge(
                back[v, last : last + 1], back[v, 0:1]
            )
        tail = p.edge_rows - p.edge_back - p.views
        if tail:
            edges_ref[slot, p.edge_back + p.views :] = jnp.zeros((tail, p.width), F32)


def payload_kernel(p, edges_ref, activity_ref, payload_ref):
    payload_ref[: p.block] = activity_ref[...].reshape(p.block, p.width)
    for e in range(p.n_edges):
        low = p.block + e * 2 * p.each
        payload_ref[low : low + 2 * p.each] = edges_ref[e, : 2 * p.each].astype(BF16)


def send_kernel(p, valid_ref, counts_ref, back_ref, values_ref, starts_ref, early_ref, *outs):
    at = lax.axis_index("view")
    row = lambda k: p.peer(at // p.pairs, k) * p.pairs + p.pairs - 1 - at % p.pairs
    last = p.slices - 1
    back = back_ref[...].astype(F32)
    for slot in range(p.n_edges):
        edge = functools.partial(edge_of, p, valid_ref, slot)
        pieces = []
        for v in range(p.views):
            for k in p.order:
                high, low = counts_ref[v, row(k), :, last, :], counts_ref[v, row(k), :, 0, :]
                pieces.append(edge(high, low).astype(F32))
        pieces += [edge(back[v, last : last + 1], back[v, 0:1]) for v in range(p.views)]
        tail = p.early_starts - p.early_back - p.views
        if tail:
            pieces.append(jnp.zeros((tail, p.width), F32))
        early_ref[slot, : p.early_starts] = jnp.concatenate(pieces, axis=0).astype(BF16)
    out = outs[0]
    values = values_ref[...].reshape(p.all_bands, p.width)
    out[p.bands : p.starts] = back_ref[...].reshape(p.views * p.slices, p.width)
    starts = jnp.concatenate([starts_ref[t] for t in range(p.taps)], axis=0)
    pieces = [lax.shift_right_logical(starts, 7), starts & 127]
    tail = p.start_rows - 2 * p.views * p.taps
    if tail:
        pieces.append(jnp.zeros((tail, p.width), I32))
    starts = jnp.concatenate(pieces, axis=0).astype(F32).astype(BF16)
    if p.split:
        lowest = valid_ref[0, 0:1, 0:1] == 0.0
        values = values.astype(F32)
        early_ref[0, p.early_starts : p.early_bands] = starts
        early_ref[0, p.early_bands :] = jnp.where(lowest, values[: p.half], values[p.half :]).astype(BF16)
    else:
        out[: p.bands] = values
        out[p.starts : p.param_rows] = starts
    put_counts(p, 0, counts_ref, out)


def put_counts(p, m, counts_ref, out):
    at = lax.axis_index("view")
    ks = p.message_peers(m)
    for v in range(p.views):
        for i, k in enumerate(ks):
            row = p.peer(at // p.pairs, k) * p.pairs + p.pairs - 1 - at % p.pairs
            low = p.base(m) + (v * len(ks) + i) * p.block
            counts = counts_ref[v, row].astype(F32).astype(BF16)
            out[low : low + p.block] = counts.reshape(p.block, p.width)


def later_kernel(p, early_ref, counts_ref, block_ref, wide_ref, half_ref, *outs):
    wide_ref[...] = early_ref[...].astype(F32)
    if p.split:
        half_ref[...] = early_ref[0, p.early_bands :]
    for i, out in enumerate(outs):
        put_counts(p, 1 + i, counts_ref, out)


def place_bands(values, start):
    width = values.shape[1]
    moved = jnp.concatenate([values, jnp.zeros((8, width), F32)], axis=0)
    for step in (1, 2, 4):
        moved = jnp.where((start & step) != 0, pltpu.roll(moved, step, 0), moved)
    step = 8
    while step < width:
        longer = min(moved.shape[0] + step, width)
        zeros = jnp.zeros((step, width), F32)
        down = jnp.concatenate([zeros, moved], axis=0)[:longer]
        stay = jnp.concatenate([moved, zeros], axis=0)[:longer]
        moved = jnp.where((start & step) != 0, down, stay)
        step *= 2
    return moved.astype(BF16)


def own_matrix_kernel(p, values_ref, starts_ref, matrix_ref):
    for v in range(p.views):
        for t in range(p.taps):
            matrix_ref[v, t] = place_bands(values_ref[v, t].astype(F32), starts_ref[t, v : v + 1])


def their_matrix_kernel(p, valid_ref, params_ref, *refs):
    matrix_ref = refs[-1]
    if p.split:
        lowest = valid_ref[0, 0:1, 0:1] == 0.0
        here, rest = params_ref[0, p.early_bands :], refs[0][...].astype(F32)
        values = [jnp.where(lowest, rest, here), jnp.where(lowest, here, rest)]
        values = jnp.concatenate(values, axis=0)
        starts = params_ref[0, p.early_starts : p.early_bands].astype(I32)
    else:
        values = params_ref[: p.bands].astype(F32)
        starts = params_ref[p.starts : p.param_rows].astype(F32).astype(I32)
    n = p.views * p.taps
    starts = starts[:n] * 128 + starts[n : 2 * n]
    for v in range(p.views):
        for t in range(p.taps):
            low, at = (v * p.taps + t) * p.band, t * p.views + v
            matrix_ref[v, t] = place_bands(values[low : low + p.band], starts[at : at + 1])


def place_source(p, blocks, lifted_ref, source_ref):
    rows = len(blocks) * p.each
    for i, block_ref in enumerate(blocks):
        low = i * p.each
        lifted_ref[low : low + p.each, 8 : 8 + p.slices, :] = (
            block_ref[: p.block].astype(F32).reshape(p.each, p.slices, p.width)
        )
        edges = block_ref[p.block :].astype(F32)
        for high, valid in enumerate(p.valid()):
            for j in range(2):
                at = (2 * min(high, p.n_edges - 1) + j) * p.each
                lifted_ref[low : low + p.each, (8 + p.slices if high else 6) + j, :] = jnp.where(
                    valid, edges[at : at + p.each], 0.0
                )
    main = rows * p.slices
    for t in range(p.taps):
        source_ref[t, :main] = (
            lifted_ref[:, 7 + t : 7 + t + p.slices, :].astype(BF16).reshape(main, p.width)
        )
        source_ref[t, main:] = jnp.concatenate(
            [lifted_ref[:, 6 + t, :], lifted_ref[:, 7 + p.slices + t, :]], axis=0
        ).astype(BF16)


class Rows:
    def __init__(self, p, stage, source_ref, ratio_ref, up_ref, down_ref):
        self.p, self.source_ref, self.ratio_ref, self.views = p, source_ref, ratio_ref, []
        self.up_ref, self.down_ref = up_ref, down_ref
        self.rows = len(p.stages[stage]) * p.each
        self.main, self.full = self.rows * p.slices, self.rows * (p.slices + 2)

    def view(self, matrix_ref, v, counts, back, edges, edge_backs):
        p, rows, main = self.p, self.rows, self.main
        expected = None
        for t in range(p.taps):
            term = jnp.dot(self.source_ref[t], matrix_ref[v, t], preferred_element_type=F32)
            expected = term if expected is None else expected + term
        inner = expected[:main].reshape(rows, p.slices, p.width) + back[None]
        ratio = counts.astype(F32).reshape(rows, p.slices, p.width) / inner - 1.0
        n = len(self.views)
        self.ratio_ref[n, :main] = ratio.astype(BF16).reshape(main, p.width)
        outer = []
        for high, valid in enumerate(p.valid()):
            low = main + high * rows
            e = min(high, p.n_edges - 1)
            ratio = edges[e] / (expected[low : low + rows] + edge_backs[e]) - 1.0
            outer.append(jnp.where(valid, ratio, 0.0))
        self.ratio_ref[n, main:] = jnp.concatenate(outer, axis=0).astype(BF16)
        self.views.append((matrix_ref, v))

    def project(self, tap, stop):
        total = None
        for n, (matrix_ref, v) in enumerate(self.views):
            term = lax.dot_general(
                self.ratio_ref[n, :stop],
                matrix_ref[v, tap],
                (((1,), (1,)), ((), ())),
                preferred_element_type=F32,
            )
            total = term if total is None else total + term
        return total

    def gradient(self):
        p, rows, main, full = self.p, self.rows, self.main, self.full
        shape = (rows, p.slices, p.width)
        part = self.project(0, full)
        self.up_ref[:, : p.slices, :] = part[:main].reshape(shape)
        self.up_ref[:, p.slices, :] = part[main + rows :]
        part = self.project(2, full)
        self.down_ref[:, 8 : 8 + p.slices, :] = part[:main].reshape(shape)
        self.down_ref[:, 7, :] = part[main : main + rows]
        total = self.project(1, main).reshape(shape)
        return total + self.up_ref[:, 1 : 1 + p.slices, :] + self.down_ref[:, 7 : 7 + p.slices, :]


def own_kernel(p, stage, counts_ref, edges_ref, back_ref, matrix_ref, *refs):
    ks = p.stages[stage]
    blocks, refs = refs[: len(ks)], refs[len(ks) :]
    refs = refs[min(stage, 1) :]
    source_ref, total_ref, lifted_ref, *scratch = refs
    place_source(p, blocks, lifted_ref, source_ref)
    work = Rows(p, stage, source_ref, *scratch)
    at = lax.axis_index("view")
    places = [p.peer(at // p.pairs, k) * p.pairs + at % p.pairs for k in ks]
    for v in range(p.views):
        edges, edge_backs = [], []
        for e in range(p.n_edges):
            pieces = []
            for row in places:
                start = p.edge_counts + (v * p.n_view + row) * p.each
                pieces.append(edges_ref[e, pl.ds(pl.multiple_of(start, p.each), p.each), :])
            edges.append(jnp.concatenate(pieces, axis=0))
            edge_backs.append(edges_ref[e, p.edge_back + v : p.edge_back + v + 1])
        counts = jnp.concatenate([counts_ref[v, row] for row in places], axis=0)
        work.view(matrix_ref, v, counts, back_ref[v].astype(F32), edges, edge_backs)
    total_ref[...] = work.gradient()


def their_kernel(p, stage, after, source_ref, total_ref, *refs):
    ks = p.stages[stage]
    refs = refs[after:]
    total = total_ref[...]
    if p.pairs == 2:
        (message_ref, first_ref, early_ref, matrix_ref), refs = refs[:4], refs[4:]
    outs, scratch = refs[: len(ks)], refs[len(ks) :]
    if p.pairs == 2:
        work = Rows(p, stage, source_ref, *scratch)
        (m,) = [m for m, stages in enumerate(p.messages) if stage in stages]
        peers = p.message_peers(m)
        skip = peers.index(ks[0])
        came = [early_ref[e].astype(F32) for e in range(p.n_edges)]
        for v in range(p.views):
            low = (v * p.line + p.order.index(ks[0])) * p.each
            edges = [x[low : low + work.rows] for x in came]
            edge_backs = [x[p.early_back + v : p.early_back + v + 1] for x in came]
            low = p.base(m) + (v * len(peers) + skip) * p.block
            back = first_ref[p.bands + v * p.slices : p.bands + (v + 1) * p.slices].astype(F32)
            counts = message_ref[low : low + work.main]
            work.view(matrix_ref, v, counts, back, edges, edge_backs)
        total = total + work.gradient()
    for i, out in enumerate(outs):
        part = total[i * p.each : (i + 1) * p.each]
        if ks[i] == 0:
            out[...] = part
        else:
            encode(p, part, out)


def encode(p, x, out_ref):
    most = jnp.maximum(jnp.max(jnp.abs(x), axis=1), 1e-30)
    power = jnp.ceil(jnp.log2(most) * STEPS)
    codes = jnp.round(x * (FULL * jnp.exp2(power * (-1.0 / STEPS)))[:, None, :])
    out_ref[: p.block] = codes.reshape(p.block, p.width).astype(I32).astype(I16)
    tail = padded_16(p.each) - p.each
    if tail:
        power = jnp.concatenate([power, jnp.zeros((tail, p.width), F32)], axis=0)
    out_ref[p.block :] = power.astype(I32).astype(I16)


def decode(p, in_ref):
    power = in_ref[p.block :].astype(I32).astype(F32)[: p.each]
    scale = jnp.exp2(power * (1.0 / STEPS)) * (1.0 / FULL)
    codes = in_ref[: p.block].astype(I32).astype(F32)
    return codes.reshape(p.each, p.slices, p.width) * scale[:, None, :]


def sum_kernel(p, coded, *refs):
    total = None
    for i, ref in enumerate(refs[:-1]):
        term = decode(p, ref) if i < coded else ref[...]
        total = term if total is None else total + term
    refs[-1][...] = total


def per_device(activity, histo_counts, background, blur_values, band_start):
    p = Plan(activity, histo_counts, blur_values)
    shape = jax.ShapeDtypeStruct
    part = lambda kernel, *static: functools.partial(kernel, p, *static)
    width = p.width
    other = [(i, i ^ 1) for i in range(p.n_view)]

    counts = histo_counts.reshape(p.views, p.n_view, p.each, p.slices, width)
    values = jnp.swapaxes(blur_values, 2, 3)
    starts = jnp.swapaxes(band_start, 0, 1)
    (valid,) = call(part(valid_kernel), [shape((2, 8, 128), F32)], flops=2 * 10**9)
    (edges,) = call(
        part(pack_kernel),
        [shape((p.n_edges, p.edge_rows, width), F32)],
        valid, counts, activity, background,
    )
    def swapped(x, flip):
        n = p.n_slab
        pairs = [(i, i ^ flip) for i in range(p.n_view)]
        up = [(i * n + s, j * n + s + 1) for i, j in pairs for s in range(n - 1)]
        down = [(i * n + s + 1, j * n + s) for i, j in pairs for s in range(n - 1)]
        send = lambda part, moves: lax.ppermute(part, ("view", "slab"), moves)
        if n > 2:
            return jnp.stack([send(x[0], up), send(x[1], down)])
        return send(x, up + down) if n == 2 else x

    outs = [shape((p.n_edges, p.early_rows, width), BF16)]
    outs += [shape((p.message_rows(0), width), BF16)]
    early, *sent = call(part(send_kernel), outs, valid, counts, background, values, starts)
    if p.pairs == 2:
        early = swapped(early, 1)
        theirs = [lax.ppermute(x, "view", other) for x in sent]
    edges = swapped(edges, 0)
    (payload,) = call(
        part(payload_kernel),
        [shape((p.block + 2 * p.n_edges * p.each, width), BF16)],
        edges, activity,
    )
    blocks = {0: payload}
    for k in [k for ks in p.stages for k in ks if k]:
        blocks[k] = lax.ppermute(payload, "view", p.across(k, False))

    if p.pairs == 2:
        outs = [shape(early.shape, F32), shape((p.half, width), BF16)]
        outs += [shape((p.message_rows(m), width), BF16) for m in range(1, len(p.messages))]
        early, rest, *later = call(part(later_kernel), outs, early, counts, blocks[p.stages[0][0]], flops=LONG)
        theirs += [lax.ppermute(x, "view", other) for x in later]
        if p.split:
            rest = swapped(rest, 0)
    matrices = shape((p.views, p.taps, width, width), BF16)
    (matrix,) = call(part(own_matrix_kernel), [matrices], values, starts)
    if p.pairs == 2:
        made_of = [early, rest] if p.split else theirs[:1]
        (their_matrix,) = call(part(their_matrix_kernel), [matrices], valid, *made_of, flops=0)

    code = shape((p.block + padded_16(p.each), width), I16)
    plain = shape((p.each, p.slices, width), F32)
    terms = {}
    for stage, ks in enumerate(p.stages):
        rows = len(ks) * p.each
        full = rows * (p.slices + 2)
        before = list(terms.values())[-1:]
        scratch = [
            pltpu.VMEM((p.views, full, width), BF16),
            pltpu.VMEM((rows, p.slices + 8, width), F32),
            pltpu.VMEM((rows, p.slices + 8, width), F32),
        ]
        own = call(
            part(own_kernel, stage),
            [shape((p.taps, full, width), BF16), shape((rows, p.slices, width), F32)],
            counts, edges, background, matrix, *[blocks[k] for k in ks], *before,
            scratch=[pltpu.VMEM((rows, p.slices + 16, width), F32)] + scratch,
            flops=LONG if stage == 0 else 4 * p.views * p.taps * full * width * width,
        )
        before = list(terms.values())[-1:]
        args = [*own, *before]
        if p.pairs == 2:
            (m,) = [m for m, stages in enumerate(p.messages) if stage in stages]
            args += [theirs[m], theirs[0], early, their_matrix]
        outs = call(
            part(their_kernel, stage, len(before)),
            [code if k else plain for k in ks],
            *args,
            scratch=[
                pltpu.VMEM((p.views, full, width), BF16),
                pltpu.VMEM((rows, p.slices + 8, width), F32),
                pltpu.VMEM((rows, p.slices + 8, width), F32),
            ],
            flops=4 * p.views * p.taps * full * width * width,
        )
        terms.update(zip(ks, outs))
    total = [terms[0]]
    for m in range(len(p.messages)):
        came = [
            lax.ppermute(terms[k], "view", p.across(k, True)) for k in p.message_peers(m)[::-1] if k
        ]
        total = list(call(part(sum_kernel, len(came)), [plain], *came, *total))
    return total[0]


def solution(mesh):
    placed = (
        P(("parts", "view"), "slab", None),
        P(("parts", "view"), None, "slab", None),
        P(("parts", "view"), "slab", None),
        P("view", None, None, None),
        P("view", None, None),
    )
    return jax.shard_map(
        per_device,
        mesh=mesh,
        in_specs=placed,
        out_specs=P(("parts", "view"), "slab", None),
        check_vma=False,
    )
```

```python
import functools

import jax
import jax.numpy as jnp
from jax import lax
from jax.experimental import pallas as pl
from jax.experimental.pallas import tpu as pltpu
from jax.sharding import PartitionSpec as P

VMEM = pl.BlockSpec(memory_space=pltpu.VMEM)
BF16, F32, I16, I32 = jnp.bfloat16, jnp.float32, jnp.int16, jnp.int32
LONG = 8 * 10**9
FULL, STEPS = 32700.0, 64.0


def padded_16(rows):
    return -(-rows // 16) * 16


class Plan:
    def __init__(self, activity, histo_counts, blur_values):
        self.each, self.slices, self.width = activity.shape
        self.views, self.taps, _, self.band = blur_values.shape
        self.n_slab = lax.axis_size("slab")
        self.n_view = lax.axis_size("view")
        self.pairs = 2 if self.n_view % 2 == 0 else 1
        self.line = self.n_view // self.pairs
        self.block = self.each * self.slices
        self.n_edges = 2 if self.n_slab > 2 else 1
        half = self.line // 2
        stages = [s for s in (range(half, self.line), range(1, half), range(1)) if len(s)]
        self.stages = [list(s) for s in stages] if half else [[0]]
        self.messages = [[0], list(range(1, len(self.stages)))][: len(self.stages)]
        self.edge_counts = 2 * self.each
        self.edge_back = self.edge_counts + self.views * self.n_view * self.each
        self.edge_rows = self.edge_back + padded_16(self.views)
        self.all_bands = self.views * self.taps * self.band
        self.start_rows = padded_16(2 * self.views * self.taps)
        self.split = self.n_slab == 2 and self.all_bands % 32 == 0
        self.bands = 0 if self.split else self.all_bands
        self.starts = self.bands + self.views * self.slices
        self.param_rows = self.starts + (0 if self.split else self.start_rows)
        self.order = [k for s in self.stages for k in s]
        self.early_back = self.views * self.line * self.each
        self.early_starts = padded_16(self.early_back + self.views)
        self.early_bands = self.early_starts + self.start_rows
        self.half = self.all_bands // 2
        self.early_rows = self.early_bands + self.half if self.split else self.early_starts

    def message_peers(self, m):
        return [k for s in self.messages[m] for k in self.stages[s]]

    def base(self, m):
        return 0 if m else self.param_rows

    def message_rows(self, m):
        return self.base(m) + self.views * len(self.message_peers(m)) * self.block

    def peer(self, at, k):
        xor = self.line & (self.line - 1) == 0
        return at ^ k if xor else (at + k) % self.line

    def across(self, k, towards):
        g = self.pairs
        moves = [(i, self.peer(i // g, k) * g + i % g) for i in range(self.n_view)]
        return moves if towards else [(j, i) for i, j in moves]

    def valid(self):
        slab = lax.axis_index("slab")
        return (slab > 0, slab < self.n_slab - 1)


def call(kernel, outs, *args, scratch=(), flops=0):
    size = lambda xs: sum(x.size * x.dtype.itemsize for x in xs)
    return pl.pallas_call(
        kernel,
        out_shape=outs,
        in_specs=[VMEM] * len(args),
        out_specs=[VMEM] * len(outs),
        scratch_shapes=list(scratch),
        compiler_params=pltpu.CompilerParams(vmem_limit_bytes=24 * 1024 * 1024),
        cost_estimate=pl.CostEstimate(
            flops=flops, bytes_accessed=size(args) + size(outs), transcendentals=0
        ),
    )(*args)


def valid_kernel(p, valid_ref):
    for high, valid in enumerate(p.valid()):
        valid_ref[high] = jnp.where(valid, jnp.ones((8, 128), F32), 0.0)


def edge_of(p, valid_ref, slot, high, low):
    if p.n_edges == 2:
        return high if slot == 0 else low
    return jnp.where(valid_ref[0, 0:1, 0:1] == 0.0, high, low)


def pack_kernel(p, valid_ref, counts_ref, activity_ref, back_ref, edges_ref):
    lowest = valid_ref[0, 0:1, 0:1] == 0.0
    last = p.slices - 1
    activity = activity_ref[...].astype(F32)
    back = back_ref[...].astype(F32)
    for slot in range(p.n_edges):

        def edge(high, low):
            if p.n_edges == 2:
                return high if slot == 0 else low
            return jnp.where(lowest, high, low)

        for j in range(2):
            edges_ref[slot, j * p.each : (j + 1) * p.each] = edge(
                activity[:, last - 1 + j, :], activity[:, j, :]
            )
        for v in range(p.views):
            for r in range(p.n_view):
                at = p.edge_counts + (v * p.n_view + r) * p.each
                edges_ref[slot, at : at + p.each] = edge(
                    counts_ref[v, r, :, last, :], counts_ref[v, r, :, 0, :]
                ).astype(F32)
            edges_ref[slot, p.edge_back + v : p.edge_back + v + 1] = edge(
                back[v, last : last + 1], back[v, 0:1]
            )
        tail = p.edge_rows - p.edge_back - p.views
        if tail:
            edges_ref[slot, p.edge_back + p.views :] = jnp.zeros((tail, p.width), F32)


def payload_kernel(p, edges_ref, activity_ref, payload_ref):
    payload_ref[: p.block] = activity_ref[...].reshape(p.block, p.width)
    for e in range(p.n_edges):
        low = p.block + e * 2 * p.each
        payload_ref[low : low + 2 * p.each] = edges_ref[e, : 2 * p.each].astype(BF16)


def send_kernel(p, valid_ref, counts_ref, back_ref, values_ref, starts_ref, early_ref, *outs):
    at = lax.axis_index("view")
    row = lambda k: p.peer(at // p.pairs, k) * p.pairs + p.pairs - 1 - at % p.pairs
    last = p.slices - 1
    back = back_ref[...].astype(F32)
    for slot in range(p.n_edges):
        edge = functools.partial(edge_of, p, valid_ref, slot)
        pieces = []
        for v in range(p.views):
            for k in p.order:
                high, low = counts_ref[v, row(k), :, last, :], counts_ref[v, row(k), :, 0, :]
                pieces.append(edge(high, low).astype(F32))
        pieces += [edge(back[v, last : last + 1], back[v, 0:1]) for v in range(p.views)]
        tail = p.early_starts - p.early_back - p.views
        if tail:
            pieces.append(jnp.zeros((tail, p.width), F32))
        early_ref[slot, : p.early_starts] = jnp.concatenate(pieces, axis=0).astype(BF16)
    out = outs[0]
    values = values_ref[...].reshape(p.all_bands, p.width)
    out[p.bands : p.starts] = back_ref[...].reshape(p.views * p.slices, p.width)
    starts = jnp.concatenate([starts_ref[t] for t in range(p.taps)], axis=0)
    pieces = [lax.shift_right_logical(starts, 7), starts & 127]
    tail = p.start_rows - 2 * p.views * p.taps
    if tail:
        pieces.append(jnp.zeros((tail, p.width), I32))
    starts = jnp.concatenate(pieces, axis=0).astype(F32).astype(BF16)
    if p.split:
        lowest = valid_ref[0, 0:1, 0:1] == 0.0
        values = values.astype(F32)
        early_ref[0, p.early_starts : p.early_bands] = starts
        early_ref[0, p.early_bands :] = jnp.where(lowest, values[: p.half], values[p.half :]).astype(BF16)
    else:
        out[: p.bands] = values
        out[p.starts : p.param_rows] = starts
    put_counts(p, 0, counts_ref, out)


def put_counts(p, m, counts_ref, out):
    at = lax.axis_index("view")
    ks = p.message_peers(m)
    for v in range(p.views):
        for i, k in enumerate(ks):
            row = p.peer(at // p.pairs, k) * p.pairs + p.pairs - 1 - at % p.pairs
            low = p.base(m) + (v * len(ks) + i) * p.block
            counts = counts_ref[v, row].astype(F32).astype(BF16)
            out[low : low + p.block] = counts.reshape(p.block, p.width)


def later_kernel(p, early_ref, counts_ref, block_ref, wide_ref, half_ref, *outs):
    wide_ref[...] = early_ref[...].astype(F32)
    if p.split:
        half_ref[...] = early_ref[0, p.early_bands :]
    for i, out in enumerate(outs):
        put_counts(p, 1 + i, counts_ref, out)


def place_bands(values, start):
    width = values.shape[1]
    moved = jnp.concatenate([values, jnp.zeros((8, width), F32)], axis=0)
    for step in (1, 2, 4):
        moved = jnp.where((start & step) != 0, pltpu.roll(moved, step, 0), moved)
    step = 8
    while step < width:
        longer = min(moved.shape[0] + step, width)
        zeros = jnp.zeros((step, width), F32)
        down = jnp.concatenate([zeros, moved], axis=0)[:longer]
        stay = jnp.concatenate([moved, zeros], axis=0)[:longer]
        moved = jnp.where((start & step) != 0, down, stay)
        step *= 2
    return moved.astype(BF16)


def own_matrix_kernel(p, values_ref, starts_ref, matrix_ref):
    for v in range(p.views):
        for t in range(p.taps):
            matrix_ref[v, t] = place_bands(values_ref[v, t].astype(F32), starts_ref[t, v : v + 1])


def their_matrix_kernel(p, valid_ref, params_ref, *refs):
    matrix_ref = refs[-1]
    if p.split:
        lowest = valid_ref[0, 0:1, 0:1] == 0.0
        here, rest = params_ref[0, p.early_bands :], refs[0][...].astype(F32)
        values = [jnp.where(lowest, rest, here), jnp.where(lowest, here, rest)]
        values = jnp.concatenate(values, axis=0)
        starts = params_ref[0, p.early_starts : p.early_bands].astype(I32)
    else:
        values = params_ref[: p.bands].astype(F32)
        starts = params_ref[p.starts : p.param_rows].astype(F32).astype(I32)
    n = p.views * p.taps
    starts = starts[:n] * 128 + starts[n : 2 * n]
    for v in range(p.views):
        for t in range(p.taps):
            low, at = (v * p.taps + t) * p.band, t * p.views + v
            matrix_ref[v, t] = place_bands(values[low : low + p.band], starts[at : at + 1])


def place_source(p, blocks, lifted_ref, source_ref):
    rows = len(blocks) * p.each
    for i, block_ref in enumerate(blocks):
        low = i * p.each
        lifted_ref[low : low + p.each, 8 : 8 + p.slices, :] = (
            block_ref[: p.block].astype(F32).reshape(p.each, p.slices, p.width)
        )
        edges = block_ref[p.block :].astype(F32)
        for high, valid in enumerate(p.valid()):
            for j in range(2):
                at = (2 * min(high, p.n_edges - 1) + j) * p.each
                lifted_ref[low : low + p.each, (8 + p.slices if high else 6) + j, :] = jnp.where(
                    valid, edges[at : at + p.each], 0.0
                )
    main = rows * p.slices
    for t in range(p.taps):
        source_ref[t, :main] = (
            lifted_ref[:, 7 + t : 7 + t + p.slices, :].astype(BF16).reshape(main, p.width)
        )
        source_ref[t, main:] = jnp.concatenate(
            [lifted_ref[:, 6 + t, :], lifted_ref[:, 7 + p.slices + t, :]], axis=0
        ).astype(BF16)


class Rows:
    def __init__(self, p, stage, source_ref, ratio_ref, up_ref, down_ref):
        self.p, self.source_ref, self.ratio_ref, self.views = p, source_ref, ratio_ref, []
        self.up_ref, self.down_ref = up_ref, down_ref
        self.rows = len(p.stages[stage]) * p.each
        self.main, self.full = self.rows * p.slices, self.rows * (p.slices + 2)

    def view(self, matrix_ref, v, counts, back, edges, edge_backs):
        p, rows, main = self.p, self.rows, self.main
        expected = None
        for t in range(p.taps):
            term = jnp.dot(self.source_ref[t], matrix_ref[v, t], preferred_element_type=F32)
            expected = term if expected is None else expected + term
        inner = expected[:main].reshape(rows, p.slices, p.width) + back[None]
        ratio = counts.astype(F32).reshape(rows, p.slices, p.width) / inner - 1.0
        n = len(self.views)
        self.ratio_ref[n, :main] = ratio.astype(BF16).reshape(main, p.width)
        outer = []
        for high, valid in enumerate(p.valid()):
            low = main + high * rows
            e = min(high, p.n_edges - 1)
            ratio = edges[e] / (expected[low : low + rows] + edge_backs[e]) - 1.0
            outer.append(jnp.where(valid, ratio, 0.0))
        self.ratio_ref[n, main:] = jnp.concatenate(outer, axis=0).astype(BF16)
        self.views.append((matrix_ref, v))

    def project(self, tap, stop):
        total = None
        for n, (matrix_ref, v) in enumerate(self.views):
            term = lax.dot_general(
                self.ratio_ref[n, :stop],
                matrix_ref[v, tap],
                (((1,), (1,)), ((), ())),
                preferred_element_type=F32,
            )
            total = term if total is None else total + term
        return total

    def gradient(self):
        p, rows, main, full = self.p, self.rows, self.main, self.full
        shape = (rows, p.slices, p.width)
        part = self.project(0, full)
        self.up_ref[:, : p.slices, :] = part[:main].reshape(shape)
        self.up_ref[:, p.slices, :] = part[main + rows :]
        part = self.project(2, main + padded_16(rows))
        self.down_ref[:, 8 : 8 + p.slices, :] = part[:main].reshape(shape)
        self.down_ref[:, 7, :] = part[main : main + rows]
        total = self.project(1, main).reshape(shape)
        return total + self.up_ref[:, 1 : 1 + p.slices, :] + self.down_ref[:, 7 : 7 + p.slices, :]


def own_kernel(p, stage, counts_ref, edges_ref, back_ref, matrix_ref, *refs):
    ks = p.stages[stage]
    blocks, refs = refs[: len(ks)], refs[len(ks) :]
    refs = refs[min(stage, 1) :]
    source_ref, total_ref, lifted_ref, *scratch = refs
    place_source(p, blocks, lifted_ref, source_ref)
    work = Rows(p, stage, source_ref, *scratch)
    at = lax.axis_index("view")
    places = [p.peer(at // p.pairs, k) * p.pairs + at % p.pairs for k in ks]
    for v in range(p.views):
        edges, edge_backs = [], []
        for e in range(p.n_edges):
            pieces = []
            for row in places:
                start = p.edge_counts + (v * p.n_view + row) * p.each
                pieces.append(edges_ref[e, pl.ds(pl.multiple_of(start, p.each), p.each), :])
            edges.append(jnp.concatenate(pieces, axis=0))
            edge_backs.append(edges_ref[e, p.edge_back + v : p.edge_back + v + 1])
        counts = jnp.concatenate([counts_ref[v, row] for row in places], axis=0)
        work.view(matrix_ref, v, counts, back_ref[v].astype(F32), edges, edge_backs)
    total_ref[...] = work.gradient()


def their_kernel(p, stage, after, source_ref, total_ref, *refs):
    ks = p.stages[stage]
    refs = refs[after:]
    total = total_ref[...]
    if p.pairs == 2:
        (message_ref, first_ref, early_ref, matrix_ref), refs = refs[:4], refs[4:]
    outs, scratch = refs[: len(ks)], refs[len(ks) :]
    if p.pairs == 2:
        work = Rows(p, stage, source_ref, *scratch)
        (m,) = [m for m, stages in enumerate(p.messages) if stage in stages]
        peers = p.message_peers(m)
        skip = peers.index(ks[0])
        came = [early_ref[e].astype(F32) for e in range(p.n_edges)]
        for v in range(p.views):
            low = (v * p.line + p.order.index(ks[0])) * p.each
            edges = [x[low : low + work.rows] for x in came]
            edge_backs = [x[p.early_back + v : p.early_back + v + 1] for x in came]
            low = p.base(m) + (v * len(peers) + skip) * p.block
            back = first_ref[p.bands + v * p.slices : p.bands + (v + 1) * p.slices].astype(F32)
            counts = message_ref[low : low + work.main]
            work.view(matrix_ref, v, counts, back, edges, edge_backs)
        total = total + work.gradient()
    for i, out in enumerate(outs):
        part = total[i * p.each : (i + 1) * p.each]
        if ks[i] == 0:
            out[...] = part
        else:
            encode(p, part, out)


def encode(p, x, out_ref):
    most = jnp.maximum(jnp.max(jnp.abs(x), axis=1), 1e-30)
    power = jnp.ceil(jnp.log2(most) * STEPS)
    codes = jnp.round(x * (FULL * jnp.exp2(power * (-1.0 / STEPS)))[:, None, :])
    out_ref[: p.block] = codes.reshape(p.block, p.width).astype(I32).astype(I16)
    tail = padded_16(p.each) - p.each
    if tail:
        power = jnp.concatenate([power, jnp.zeros((tail, p.width), F32)], axis=0)
    out_ref[p.block :] = power.astype(I32).astype(I16)


def decode(p, in_ref):
    power = in_ref[p.block :].astype(I32).astype(F32)[: p.each]
    scale = jnp.exp2(power * (1.0 / STEPS)) * (1.0 / FULL)
    codes = in_ref[: p.block].astype(I32).astype(F32)
    return codes.reshape(p.each, p.slices, p.width) * scale[:, None, :]


def sum_kernel(p, coded, *refs):
    total = None
    for i, ref in enumerate(refs[:-1]):
        term = decode(p, ref) if i < coded else ref[...]
        total = term if total is None else total + term
    refs[-1][...] = total


def per_device(activity, histo_counts, background, blur_values, band_start):
    p = Plan(activity, histo_counts, blur_values)
    shape = jax.ShapeDtypeStruct
    part = lambda kernel, *static: functools.partial(kernel, p, *static)
    width = p.width
    other = [(i, i ^ 1) for i in range(p.n_view)]

    counts = histo_counts.reshape(p.views, p.n_view, p.each, p.slices, width)
    values = jnp.swapaxes(blur_values, 2, 3)
    starts = jnp.swapaxes(band_start, 0, 1)
    (valid,) = call(part(valid_kernel), [shape((2, 8, 128), F32)], flops=2 * 10**9)
    (edges,) = call(
        part(pack_kernel),
        [shape((p.n_edges, p.edge_rows, width), F32)],
        valid, counts, activity, background,
    )
    def swapped(x, flip):
        n = p.n_slab
        pairs = [(i, i ^ flip) for i in range(p.n_view)]
        up = [(i * n + s, j * n + s + 1) for i, j in pairs for s in range(n - 1)]
        down = [(i * n + s + 1, j * n + s) for i, j in pairs for s in range(n - 1)]
        send = lambda part, moves: lax.ppermute(part, ("view", "slab"), moves)
        if n > 2:
            return jnp.stack([send(x[0], up), send(x[1], down)])
        return send(x, up + down) if n == 2 else x

    outs = [shape((p.n_edges, p.early_rows, width), BF16)]
    outs += [shape((p.message_rows(0), width), BF16)]
    early, *sent = call(part(send_kernel), outs, valid, counts, background, values, starts)
    if p.pairs == 2:
        early = swapped(early, 1)
        theirs = [lax.ppermute(x, "view", other) for x in sent]
    edges = swapped(edges, 0)
    (payload,) = call(
        part(payload_kernel),
        [shape((p.block + 2 * p.n_edges * p.each, width), BF16)],
        edges, activity,
    )
    blocks = {0: payload}
    for k in [k for ks in p.stages for k in ks if k]:
        blocks[k] = lax.ppermute(payload, "view", p.across(k, False))

    if p.pairs == 2:
        outs = [shape(early.shape, F32), shape((p.half, width), BF16)]
        outs += [shape((p.message_rows(m), width), BF16) for m in range(1, len(p.messages))]
        early, rest, *later = call(part(later_kernel), outs, early, counts, blocks[p.stages[0][0]], flops=LONG)
        theirs += [lax.ppermute(x, "view", other) for x in later]
        if p.split:
            rest = swapped(rest, 0)
    matrices = shape((p.views, p.taps, width, width), BF16)
    (matrix,) = call(part(own_matrix_kernel), [matrices], values, starts)
    if p.pairs == 2:
        made_of = [early, rest] if p.split else theirs[:1]
        (their_matrix,) = call(part(their_matrix_kernel), [matrices], valid, *made_of, flops=0)

    code = shape((p.block + padded_16(p.each), width), I16)
    plain = shape((p.each, p.slices, width), F32)
    terms = {}
    for stage, ks in enumerate(p.stages):
        rows = len(ks) * p.each
        full = rows * (p.slices + 2)
        before = list(terms.values())[-1:]
        scratch = [
            pltpu.VMEM((p.views, full, width), BF16),
            pltpu.VMEM((rows, p.slices + 8, width), F32),
            pltpu.VMEM((rows, p.slices + 8, width), F32),
        ]
        own = call(
            part(own_kernel, stage),
            [shape((p.taps, full, width), BF16), shape((rows, p.slices, width), F32)],
            counts, edges, background, matrix, *[blocks[k] for k in ks], *before,
            scratch=[pltpu.VMEM((rows, p.slices + 16, width), F32)] + scratch,
            flops=LONG if stage == 0 else 4 * p.views * p.taps * full * width * width,
        )
        before = list(terms.values())[-1:]
        args = [*own, *before]
        if p.pairs == 2:
            (m,) = [m for m, stages in enumerate(p.messages) if stage in stages]
            args += [theirs[m], theirs[0], early, their_matrix]
        outs = call(
            part(their_kernel, stage, len(before)),
            [code if k else plain for k in ks],
            *args,
            scratch=[
                pltpu.VMEM((p.views, full, width), BF16),
                pltpu.VMEM((rows, p.slices + 8, width), F32),
                pltpu.VMEM((rows, p.slices + 8, width), F32),
            ],
            flops=4 * p.views * p.taps * full * width * width,
        )
        terms.update(zip(ks, outs))
    total = [terms[0]]
    for m in range(len(p.messages)):
        came = [
            lax.ppermute(terms[k], "view", p.across(k, True)) for k in p.message_peers(m)[::-1] if k
        ]
        total = list(call(part(sum_kernel, len(came)), [plain], *came, *total))
    return total[0]


def solution(mesh):
    placed = (
        P(("parts", "view"), "slab", None),
        P(("parts", "view"), None, "slab", None),
        P(("parts", "view"), "slab", None),
        P("view", None, None, None),
        P("view", None, None),
    )
    return jax.shard_map(
        per_device,
        mesh=mesh,
        in_specs=placed,
        out_specs=P(("parts", "view"), "slab", None),
        check_vma=False,
    )
```
